1024 devices in a mesh: expert: 64 (over x_hi, z, core), context: 16 (over y, x_lo).
Axes of the slice: x: 8 (x_hi: 4, x_lo: 2; x = x_hi * 2 + x_lo), y: 8, z: 8, core: 2. Of those that a mesh axis runs over, the one named last changes fastest.
Arguments:
- queries: bfloat16 [64, 16, 4096], P('expert', None, 'context'), may hold values from -2.5 to 2.5
- keys_values: bfloat16 [64, 2048, 512], P('expert', 'context'), may hold values from -2.5 to 2.5
- out_proj: bfloat16 [4096, 4096], P('context'), may hold values from -0.09375 to 0.09375
- norm_gain: float32 [4096], P('context'), may hold values from 0.5 to 2
- expert_ids: int32 [64, 16, 8], P('expert'), may hold values from 0 to 63, all different within a row; in each aligned block of 16 rows (0 to 15, 16 to 31, ..., all dimensions but the last counted through in order) at most 3 rows name the same one
- route_logits: float32 [64, 16, 8], P('expert'), may hold values from -6 to 6
- home: int32 [64], replicated, may hold values from 0 to 63, each once
- gate_up: bfloat16 [64, 4096, 3072], P('expert', 'context'), may hold values from -0.09375 to 0.09375
- down: bfloat16 [64, 1536, 4096], P('expert', None, 'context'), may hold values from -0.15625 to 0.15625
Outputs:
- moe_out: bfloat16 [64, 16, 4096], P('expert', None, 'context')
The draws below stay inside these ranges and needn't reach their ends.
Inputs may be any that keep to these rules, and one draw needn't show every extreme that they name: `expert_ids`: in each sequence's 16 rows no expert is named by more than 3 rows, a bound that some block reaches. `home`: each slot holds exactly one expert.
All inputs are finite; a program needn't handle non-finite values.
Results may differ from the reference program's by a relative error of at most 0.04.
Values may be sent and summed in bfloat16 or wider, within the bound.
A program may use at most 32 MiB of HBM per device.

```python
import math
import jax
import jax.numpy as jnp
import numpy as np
from jax import lax

D = 4096
FF = 1536
HQ = 32
HD = 128
KVH = 2
EXPERTS = 64
TOPK = 8
MROWS = 16
CAP = 3
SEQS = 64
LENGTH = 2048
N_CONTEXT = 16


def levels(stream_key, dims, split, smallest, largest):
    level = 1.0
    for axis_at, shards_of in split:
        draws = jax.random.uniform(jax.random.fold_in(jax.random.fold_in(stream_key, 6), axis_at), (shards_of,), jnp.float32, smallest / len(split), largest / len(split))
        level = level * jnp.repeat(jnp.exp(draws), dims[axis_at] // shards_of).reshape((-1,) + (1,) * (len(dims) - 1 - axis_at))
    return level


def deal_out(key, own, number, rows, count, top, most, lean):
    sequence = jax.random.permutation(key, count)
    crowded, common = shares(count, rows * top, most, lean, True), shares(count, rows * top, most, lean, False)
    places = jnp.arange(count)

    def named(sizes, offset_by):
        used = int((sizes > 0).sum())
        fixed = max(1, used // 4)
        shifted = fixed + (places - fixed + offset_by * (used - fixed)) % max(1, count - fixed)
        return jnp.zeros((count,), jnp.int32).at[sequence[jnp.where(places < fixed, places, shifted)]].set(jnp.asarray(sizes, jnp.int32))

    sizes = jnp.where(number % 4 == 0, named(crowded, number // 4), named(common, number - number // 4 - 1))
    mixed = jax.random.permutation(jax.random.fold_in(own, 3), count)
    source_of, taker = mixed[0:count // 2 * 2:2], mixed[1:count // 2 * 2:2]
    slack = jnp.minimum(sizes[source_of] - 1, most - sizes[taker]) // 2
    slack = jnp.where((source_of == sequence[0]) | (taker == sequence[0]) | (sizes[taker] == 0), 0, jnp.maximum(slack, 0))
    shifted = jax.random.randint(jax.random.fold_in(own, 4), (count // 2,), 0, 1 << 20) % (slack + 1)
    sizes = sizes.at[source_of].add(-shifted).at[taker].add(shifted)
    labels = jnp.searchsorted(jnp.cumsum(sizes), jnp.arange(rows * top), side="right").astype(jnp.int32)
    listing = labels.reshape(top, rows).T
    listing = listing[jax.random.permutation(jax.random.fold_in(own, 1), rows)]
    offset_by = jax.random.randint(jax.random.fold_in(own, 2), (rows, 1), 0, top)
    return jnp.take_along_axis(listing, (jnp.arange(top)[None, :] + offset_by) % top, axis=1)


def shares(number_of, total, bound, slope, full):
    weights = [(1 << 20) // math.isqrt(grade ** slope) + 1 for grade in range(1, number_of + 1)]
    largest = bound if full else min(bound, max(-(-total // number_of), total * weights[0] // sum(weights)))
    least = 1 if total - largest >= number_of - 1 else 0
    holding, surplus = [largest] + [least] * (number_of - 1), total - largest - least * (number_of - 1)
    while surplus > 0:
        free = [i for i in range(1, number_of) if holding[i] < largest] or [i for i in range(1, number_of) if holding[i] < bound]
        pool, budget = sum([weights[i] for i in free]), surplus
        for i in free:
            extra = min(bound - holding[i], max(1, budget * weights[i] // pool), surplus)
            holding[i] = holding[i] + extra
            surplus = surplus - extra
    return np.array(holding)


def noise(key, extent, scale, most, cuts=(), kind=jnp.bfloat16):
    values = scale * jax.random.normal(key, extent, jnp.float32)
    if cuts:
        values = values * levels(key, extent, cuts, -0.22, 0.18)
    return jnp.clip(values, -most, most).astype(kind)


def setup_inputs(seed: int = 0) -> dict:
    streams_of = jax.random.split(jax.random.key(seed), 10)
    queries = noise(streams_of[0], (SEQS, MROWS, HQ * HD), 1.0, 2.5, ((0, 64), (2, 16)))
    keys_values = noise(streams_of[1], (SEQS, LENGTH, 2 * KVH * HD), 1.0, 2.5, ((0, 64), (1, 16)))
    out_proj = noise(streams_of[2], (HQ * HD, D), (HQ * HD) ** -0.5, 0.09375, ((0, 16),))
    norm_gain = jnp.clip(jnp.exp(math.log(2.0) - 1.3862944 * jax.random.uniform(streams_of[3], (D,), jnp.float32) ** levels(streams_of[3], (D,), ((0, 16),), -0.2, 0.2)), 0.5, 2.0)
    expert_ids_keys = jax.random.split(jax.random.fold_in(streams_of[4], 1), SEQS * MROWS // MROWS)
    expert_ids_turns = jax.random.permutation(jax.random.fold_in(streams_of[4], 3), SEQS * MROWS // MROWS)
    expert_ids = jax.vmap(lambda own, number: deal_out(jax.random.fold_in(streams_of[4], 2), own, number, MROWS, EXPERTS, TOPK, CAP, 2))(expert_ids_keys, expert_ids_turns).reshape((SEQS, MROWS, TOPK))
    route_logits = noise(streams_of[5], (SEQS, MROWS, TOPK), 1.5, 6.0, ((0, 64),), jnp.float32)
    home = jax.random.permutation(streams_of[6], EXPERTS).astype(jnp.int32)
    gate_up = noise(streams_of[7], (EXPERTS, D, 2 * FF), D ** -0.5, 0.09375, ((0, 64), (1, 16)))
    down = noise(streams_of[8], (EXPERTS, FF, D), FF ** -0.5, 0.15625, ((0, 64), (2, 16)))
    return {"queries": queries, "keys_values": keys_values, "out_proj": out_proj, "norm_gain": norm_gain, "expert_ids": expert_ids, "route_logits": route_logits, "home": home, "gate_up": gate_up, "down": down}


def slot_tables(expert_row, home):
    slot = lax.optimization_barrier(jnp.sum((expert_row[:, :, None] == jnp.arange(EXPERTS, dtype=jnp.int32)).astype(jnp.int32) * home[None, None, :], axis=2)).astype(jnp.int32)
    flat = slot.reshape(-1)
    onehot = (flat[:, None] == jnp.arange(EXPERTS, dtype=jnp.int32)).astype(jnp.int32)
    before = jnp.cumsum(onehot, axis=0) - onehot
    rank = lax.optimization_barrier(jnp.sum(before * onehot, axis=1)).astype(jnp.int32)
    place = (flat * CAP + rank).astype(jnp.int32)
    table = place[:, None] == jnp.arange(EXPERTS * CAP, dtype=jnp.int32)
    return table.reshape(MROWS, TOPK, EXPERTS * CAP)

def attend_sequence(args):
    query, pairs = args
    group = HQ // KVH
    qfull = query.astype(jnp.float32).reshape(MROWS, KVH, group, HD)
    keys = pairs[:, :KVH * HD].astype(jnp.float32).reshape(LENGTH, KVH, HD)
    values = pairs[:, KVH * HD:].astype(jnp.float32).reshape(LENGTH, KVH, HD)
    scores = jnp.einsum('igkd,tgd->igkt', qfull, keys) * HD ** (-0.5)
    stride = LENGTH // MROWS
    qpos = (jnp.arange(MROWS, dtype=jnp.int32) + 1) * stride - 1
    visible = jnp.arange(LENGTH, dtype=jnp.int32)[None, :] <= qpos[:, None]
    weight = jnp.where(visible[:, None, None, :], jnp.exp(scores), 0.0)
    denom = lax.optimization_barrier(jnp.sum(weight, axis=-1))
    weight_low = weight.astype(jnp.bfloat16).astype(jnp.float32)
    numer = jnp.einsum('igkt,tgd->igkd', weight_low, values)
    return (numer / denom[..., None]).reshape(MROWS, HQ * HD)

def reference(queries, keys_values, out_proj, norm_gain, expert_ids, route_logits, home, gate_up, down):
    attended = lax.map(attend_sequence, (queries, keys_values)).astype(jnp.bfloat16)
    projected = jnp.dot(attended.reshape(SEQS * MROWS, HQ * HD), out_proj, preferred_element_type=jnp.float32).reshape(SEQS, MROWS, D)
    normed_in = (projected * norm_gain).astype(jnp.bfloat16)
    width = D // N_CONTEXT
    square_parts = lax.optimization_barrier(jnp.sum((projected * projected).reshape(SEQS, MROWS, N_CONTEXT, width), axis=3)).astype(jnp.bfloat16)
    raised = jnp.exp(route_logits)
    route_low = (raised / lax.optimization_barrier(jnp.sum(raised, axis=-1, keepdims=True))).astype(jnp.bfloat16)
    tables = jax.vmap(slot_tables, in_axes=(0, None))(expert_ids, home)
    picks = lax.optimization_barrier(jnp.sum(tables.astype(jnp.float32), axis=2))
    slot_rows = jnp.einsum('bip,bid->bpd', picks, normed_in.astype(jnp.float32)).astype(jnp.bfloat16)
    slot_squares = jnp.einsum('bip,bic->bpc', picks, square_parts.astype(jnp.float32))
    slot_rows = jnp.moveaxis(slot_rows.reshape(SEQS, EXPERTS, CAP, D), 1, 0)
    slot_squares = jnp.moveaxis(slot_squares.reshape(SEQS, EXPERTS, CAP, N_CONTEXT), 1, 0)

    def run_expert(args):
        rows, squares, weight_in, weight_out = args
        parts = jnp.einsum('rcd,cdf->rcf', rows.reshape(SEQS * CAP, N_CONTEXT, width).astype(jnp.float32), weight_in.reshape(N_CONTEXT, width, 2 * FF).astype(jnp.float32))
        parts = lax.optimization_barrier(parts.astype(jnp.bfloat16))
        total = lax.optimization_barrier(jnp.sum(parts.astype(jnp.float32), axis=1))
        scale = lax.rsqrt(lax.optimization_barrier(jnp.sum(squares.reshape(SEQS * CAP, N_CONTEXT), axis=1)) / D + 1e-06)
        gate = scale[:, None] * total[:, :FF]
        upper = scale[:, None] * total[:, FF:]
        hidden_act = (jax.nn.silu(gate) * upper).astype(jnp.bfloat16)
        result = jnp.dot(hidden_act, weight_out, preferred_element_type=jnp.float32).astype(jnp.bfloat16)
        return result.reshape(SEQS, CAP, D)
    expert_out = lax.map(run_expert, (slot_rows, slot_squares, gate_up, down))
    gathered = jnp.moveaxis(expert_out, 0, 1).reshape(SEQS, EXPERTS * CAP, D)
    combine = lax.optimization_barrier(jnp.sum(tables.astype(jnp.float32) * route_low.astype(jnp.float32)[..., None], axis=2))
    moe_out = jnp.einsum('bip,bpd->bid', combine, gathered.astype(jnp.float32)).astype(jnp.bfloat16)
    return moe_out
```

```python
import functools

import jax
import jax.numpy as jnp
from jax import lax
from jax.experimental import pallas as pl
from jax.experimental.pallas import tpu as pltpu
from jax.sharding import PartitionSpec as P

MESH = pl.DeviceIdType.MESH
BF = jnp.bfloat16
F32 = jnp.float32

D = 4096
FF = 1536
HD = 128
MROWS = 16
TOPK = 8
CTX = 16
NY = 8
NZ = 8
NXC = 8
SLOTS = 256
ROWS = 192
RB = 48
CB = 384
CHUNK = 6 * RB + 16
SEND_ORDER = [(dy, dx) for dy in (4, 3, 5, 2, 6, 1, 7, 0) for dx in (1, 0) if (dy, dx) != (0, 0)]


def iota(shape, dim):
    return lax.broadcasted_iota(jnp.int32, shape, dim)


def dot(a, b, ca=1, cb=0):
    return lax.dot_general(a, b, (((ca,), (cb,)), ((), ())), preferred_element_type=F32)


def kernel(
    q_ref, kv_hbm, op_hbm, gain_ref, ids_ref, logits_ref, home_ref, gu_hbm, dn_hbm, out_ref,
    kv, op, gu, dn, qall, nb, nr, cs, cr, d1s, d1r, d2s, d2r, es, er, acc, fs, hid, g1s, g1r, g2s, g2r,
    picks_ref, combine_ref, perm_ref,
    load_sem, send_sem, q_sem, n_sem, c_sem, d1_sem, d2_sem, e_sem, fsend_sem, f_sem, g1_sem, g2_sem,
):
    e = lax.axis_index("expert")
    c = lax.axis_index("context")
    y, xl = c // 2, c % 2
    core, z, xh = e % 2, (e // 2) % NZ, e // (2 * NZ)
    xc = xh * 2 + core

    loads = [
        pltpu.make_async_copy(src, dst, load_sem.at[i])
        for i, (src, dst) in enumerate([(kv_hbm.at[0], kv), (op_hbm, op), (gu_hbm.at[0], gu), (dn_hbm.at[0], dn)])
    ]
    for load in loads:
        load.start()

    def ctx_peer(dy, dx):
        return ((y + dy) % NY) * 2 + (xl + dx) % 2

    def z_peer(d):
        other = (z + d) % NZ
        return other, (xh * NZ + other) * 2 + core

    def xc_peer(d):
        other = (xc + d) % NXC
        return other, ((other // 2) * NZ + z) * 2 + other % 2

    barrier = pltpu.get_barrier_semaphore()

    def greet(ee, cc):
        pl.semaphore_signal(barrier, inc=1, device_id=(ee, cc), device_id_type=MESH)

    for dy, dx in SEND_ORDER:
        greet(e, ctx_peer(dy, dx))
    for d in range(1, 8):
        greet(z_peer(d)[1], c)
        greet(xc_peer(d)[1], c)

    ids = ids_ref[0]
    logits = logits_ref[0]
    raised = jnp.exp(logits)
    route = (raised / jnp.sum(raised, axis=1, keepdims=True)).astype(BF).astype(F32)
    lanes = iota((MROWS, 64), 1)
    chosen = jnp.zeros((MROWS, 64), F32)
    weights = jnp.zeros((MROWS, 64), F32)
    for j in range(TOPK):
        hit = ids[:, j : j + 1] == lanes
        chosen = chosen + jnp.where(hit, 1.0, 0.0)
        weights = weights + jnp.where(hit, route[:, j : j + 1], 0.0)
    r = iota((SLOTS, 64), 0)
    r_xc = (r >> 2) & 7
    r_slot = ((r_xc >> 1) * NZ + (r >> 5)) * 2 + (r_xc & 1)
    lands = jnp.where(home_ref[...] == r_slot, 1.0, 0.0).astype(BF)
    chosen_r = dot(chosen.astype(BF), lands, 1, 1)
    weights_r = dot(weights.astype(BF), lands, 1, 1)
    earlier = jnp.where(iota((MROWS, MROWS), 1) < iota((MROWS, MROWS), 0), 1.0, 0.0).astype(BF)
    rank = dot(earlier, chosen_r.astype(BF))
    right_rank = rank == (iota((MROWS, SLOTS), 1) & 3).astype(F32)
    picks_ref[...] = jnp.where(right_rank, chosen_r, 0.0).astype(BF)
    combine_ref[...] = jnp.where(right_rank, weights_r, 0.0).astype(BF)
    pr, pc = iota((SLOTS, SLOTS), 0), iota((SLOTS, SLOTS), 1)
    perm_ref[...] = jnp.where(pc == ((pr >> 2) & 7) * 32 + (pr >> 5) * 4 + (pr & 3), 1.0, 0.0).astype(BF)

    qall[c] = q_ref[0]
    pl.semaphore_wait(barrier, 29)

    def send(src, dst, s_sem, r_sem, ee, cc):
        pltpu.make_async_remote_copy(
            src_ref=src, dst_ref=dst, send_sem=s_sem, recv_sem=r_sem, device_id=(ee, cc), device_id_type=MESH
        ).start()

    def await_bytes(ref, sem):
        pltpu.make_async_copy(ref, ref, sem).wait()

    for dy, dx in SEND_ORDER:
        send(q_ref.at[0], qall.at[c], send_sem.at[0], q_sem, e, ctx_peer(dy, dx))
    loads[0].wait()
    await_bytes(qall.at[pl.ds(0, 15)], q_sem)

    visible = (iota((128, 128), 0) & 15) >= c
    for g in range(2):
        key, value = kv[:, g * HD : (g + 1) * HD], kv[:, (2 + g) * HD : (3 + g) * HD]
        denoms = []
        for p in range(2):
            query = qall[8 * g : 8 * g + 8, :, p * HD : (p + 1) * HD].reshape(128, HD)
            scores = dot(query, key, 1, 1) * HD ** (-0.5)
            weight = jnp.where(visible, jnp.exp(scores), 0.0)
            denoms.append(jnp.sum(weight, axis=1, keepdims=True))
            numer = dot(weight.astype(BF), value)
            nb[8 * g : 8 * g + 8, :, p * HD : (p + 1) * HD] = numer.astype(BF).reshape(8, MROWS, HD)
        lane = iota((128, 128), 1)
        both = jnp.where(lane < 64, denoms[0], denoms[1])
        high = both.astype(BF).astype(F32)
        packed = jnp.where((lane & 63) < 32, high, both - high)
        nb[8 * g : 8 * g + 8, :, 256:384] = packed.astype(BF).reshape(8, MROWS, 128)

    for dy, dx in SEND_ORDER:
        peer = ctx_peer(dy, dx)
        send(nb.at[peer], nr.at[dy * 2 + dx], send_sem.at[1], n_sem, e, peer)
    nr[0] = nb[c]
    await_bytes(nr.at[pl.ds(1, 15)], n_sem)
    total = nr[0].astype(F32)
    for j in range(1, CTX):
        total = total + nr[j].astype(F32)
    denom0 = total[:, 256:257] + total[:, 288:289]
    denom1 = total[:, 320:321] + total[:, 352:353]
    attended = jnp.concatenate([total[:, 0:128] / denom0, total[:, 128:256] / denom1], axis=1).astype(BF)

    loads[1].wait()
    for dy, dx in SEND_ORDER + [(0, 0)]:
        peer = ctx_peer(dy, dx)
        j = dy * 2 + dx
        part = dot(attended, op[:, pl.ds(pl.multiple_of(peer * 256, 256), 256)]).astype(BF)
        if j == 0:
            cr[0] = part
        else:
            cs[j] = part
            send(cs.at[j], cr.at[j], send_sem.at[2], c_sem, e, peer)
    await_bytes(cr.at[pl.ds(1, 15)], c_sem)
    projected = cr[0].astype(F32)
    for j in range(1, CTX):
        projected = projected + cr[j].astype(F32)
    gain = gain_ref[...]
    normed = (projected * gain).astype(BF)

    d1s[...] = dot(picks_ref[...], normed, 0, 0).astype(BF).reshape(NZ, 32, 256)
    for d in (4, 3, 5, 2, 6, 1, 7):
        other, peer = z_peer(d)
        send(d1s.at[other], d1r.at[z], send_sem.at[3], d1_sem, peer, c)
    d1r[z] = d1s[z]
    await_bytes(d1r.at[pl.ds(0, 7)], d1_sem)
    d2s[...] = dot(perm_ref[...], d1r[...].reshape(SLOTS, 256)).astype(BF).reshape(NXC, 32, 256)
    for d in (4, 3, 5, 2, 6, 1, 7):
        other, peer = xc_peer(d)
        send(d2s.at[other], d2r.at[xc], send_sem.at[4], d2_sem, peer, c)
    d2r[xc] = d2s[xc]
    squeeze = jnp.where(
        iota((ROWS, SLOTS), 1) == (iota((ROWS, SLOTS), 0) & 63) * 4 + (iota((ROWS, SLOTS), 0) >> 6), 1.0, 0.0
    ).astype(BF)
    await_bytes(d2r.at[pl.ds(0, 7)], d2_sem)
    rows32 = dot(squeeze, d2r[...].reshape(SLOTS, 256))
    rows = rows32.astype(BF)

    raw = rows32 * (1.0 / gain)
    squares = jnp.sum(raw * raw, axis=1, keepdims=True)
    lane16 = iota((16, 128), 1)
    tiles = []
    for rb in range(4):
        a, b, cc = (squares[rb * RB + t * 16 : rb * RB + t * 16 + 16] for t in range(3))
        tiles.append(jnp.where(lane16 < 32, a, jnp.where(lane16 < 64, b, cc)).astype(BF))
    loads[2].wait()
    my_cb = c // 4
    for step in (2, 1, 3, 0):
        cb = (my_cb + step) % 4
        for half in range(2):
            start = pl.multiple_of(half * FF + cb * CB, 128)
            part = dot(rows, gu[:, pl.ds(start, CB)]).astype(BF)
            for rb in range(4):
                for t in range(3):
                    at = (half * 3 + t) * RB
                    es[cb * 4 + rb, at : at + RB, :] = part[rb * RB : rb * RB + RB, t * 128 : t * 128 + 128]
        for rb in range(4):
            es[cb * 4 + rb, 6 * RB : CHUNK, :] = tiles[rb]
        for rb in range(4):
            peer = cb * 4 + rb
            slot = ((peer // 2 - y) % NY) * 2 + (peer + xl) % 2

            @pl.when(peer != c)
            def _():
                send(es.at[peer], er.at[slot], send_sem.at[5], e_sem.at[slot], e, peer)

    acc[...] = es[c].astype(F32)
    for n, (dy, dx) in enumerate(SEND_ORDER):
        j = dy * 2 + dx
        await_bytes(er.at[j], e_sem.at[j])
        acc[...] += er[j].astype(F32)
    scale16 = lax.rsqrt(acc[6 * RB : CHUNK, :] * (1.0 / D) + 1e-06)
    scale = jnp.concatenate([scale16[:, 0:1], scale16[:, 32:33], scale16[:, 64:65]], axis=0)
    for t in range(3):
        gate = acc[t * RB : t * RB + RB, :] * scale
        upper = acc[(3 + t) * RB : (4 + t) * RB, :] * scale
        fs[:, t * 128 : t * 128 + 128] = (gate / (1.0 + jnp.exp(-gate)) * upper).astype(BF)
    row_at = pl.multiple_of((c % 4) * RB, 16)
    col_at = pl.multiple_of(my_cb * CB, 128)
    mine = hid.at[pl.ds(row_at, RB), pl.ds(col_at, CB)]
    for dy, dx in SEND_ORDER:
        send(fs, mine, fsend_sem.at[dy * 2 + dx], f_sem.at[dy * 2 + dx], e, ctx_peer(dy, dx))
    hid[pl.ds(row_at, RB), pl.ds(col_at, CB)] = fs[...]
    stretch = jnp.where(
        iota((SLOTS, ROWS), 0) == (iota((SLOTS, ROWS), 1) & 63) * 4 + (iota((SLOTS, ROWS), 1) >> 6), 1.0, 0.0
    ).astype(BF)
    loads[3].wait()
    for dy, dx in SEND_ORDER:
        await_bytes(fs, f_sem.at[dy * 2 + dx])
    result = dot(hid[...], dn[...]).astype(BF)

    g1s[...] = dot(stretch, result).astype(BF).reshape(NXC, 32, 256)
    for d in (4, 3, 5, 2, 6, 1, 7):
        other, peer = xc_peer(d)
        send(g1s.at[other], g1r.at[xc], send_sem.at[7], g1_sem, peer, c)
    g1r[xc] = g1s[xc]
    await_bytes(g1r.at[pl.ds(0, 7)], g1_sem)
    g2s[...] = dot(perm_ref[...], g1r[...].reshape(SLOTS, 256)).astype(BF).reshape(NZ, 32, 256)
    for d in (4, 3, 5, 2, 6, 1, 7):
        other, peer = z_peer(d)
        send(g2s.at[other], g2r.at[z], send_sem.at[8], g2_sem, peer, c)
    g2r[z] = g2s[z]
    await_bytes(g2r.at[pl.ds(0, 7)], g2_sem)
    out_ref[0] = dot(combine_ref[...], g2r[...].reshape(SLOTS, 256)).astype(BF)

    await_bytes(qall.at[pl.ds(0, 15)], send_sem.at[0])
    await_bytes(nr.at[pl.ds(0, 15)], send_sem.at[1])
    await_bytes(cr.at[pl.ds(0, 15)], send_sem.at[2])
    await_bytes(d1r.at[pl.ds(0, 7)], send_sem.at[3])
    await_bytes(d2r.at[pl.ds(0, 7)], send_sem.at[4])
    await_bytes(er.at[pl.ds(0, 15)], send_sem.at[5])
    for j in range(1, CTX):
        await_bytes(fs, fsend_sem.at[j])
    await_bytes(g1r.at[pl.ds(0, 7)], send_sem.at[7])
    await_bytes(g2r.at[pl.ds(0, 7)], send_sem.at[8])


def body(queries, keys_values, out_proj, norm_gain, expert_ids, route_logits, home, gate_up, down):
    vm = pl.BlockSpec(memory_space=pltpu.VMEM)
    hb = pl.BlockSpec(memory_space=pl.ANY)
    dma = pltpu.SemaphoreType.DMA
    vmem = pltpu.VMEM
    return pl.pallas_call(
        kernel,
        out_shape=jax.ShapeDtypeStruct((1, MROWS, 256), BF),
        in_specs=[vm, hb, hb, vm, vm, vm, vm, hb, hb],
        out_specs=vm,
        scratch_shapes=[
            vmem((128, 512), BF),
            vmem((256, D), BF),
            vmem((256, 2 * FF), BF),
            vmem((FF, 256), BF),
            vmem((CTX, MROWS, 256), BF),
            vmem((CTX, MROWS, 384), BF),
            vmem((CTX, MROWS, 384), BF),
            vmem((CTX, MROWS, 256), BF),
            vmem((CTX, MROWS, 256), BF),
            vmem((NZ, 32, 256), BF),
            vmem((NZ, 32, 256), BF),
            vmem((NXC, 32, 256), BF),
            vmem((NXC, 32, 256), BF),
            vmem((CTX, CHUNK, 128), BF),
            vmem((CTX, CHUNK, 128), BF),
            vmem((CHUNK, 128), F32),
            vmem((RB, CB), BF),
            vmem((ROWS, FF), BF),
            vmem((NXC, 32, 256), BF),
            vmem((NXC, 32, 256), BF),
            vmem((NZ, 32, 256), BF),
            vmem((NZ, 32, 256), BF),
            vmem((MROWS, SLOTS), BF),
            vmem((MROWS, SLOTS), BF),
            vmem((SLOTS, SLOTS), BF),
            dma((4,)),
            dma((9,)),
            dma, dma, dma, dma, dma,
            dma((CTX,)),
            dma((CTX,)),
            dma((CTX,)),
            dma, dma,
        ],
        compiler_params=pltpu.CompilerParams(
            collective_id=0, has_side_effects=True, vmem_limit_bytes=40 * 1024 * 1024
        ),
    )(
        queries, keys_values, out_proj, norm_gain.reshape(1, 256), expert_ids, route_logits,
        home.reshape(1, 64), gate_up, down,
    )


def solution(mesh):
    in_specs = (
        P("expert", None, "context"),
        P("expert", "context", None),
        P("context", None),
        P("context"),
        P("expert", None, None),
        P("expert", None, None),
        P(),
        P("expert", "context", None),
        P("expert", None, "context"),
    )
    out_specs = P("expert", None, "context")
    return jax.shard_map(body, mesh=mesh, in_specs=in_specs, out_specs=out_specs, check_vma=False)
```

```python
import functools

import jax
import jax.numpy as jnp
from jax import lax
from jax.experimental import pallas as pl
from jax.experimental.pallas import tpu as pltpu
from jax.sharding import PartitionSpec as P

MESH = pl.DeviceIdType.MESH
BF = jnp.bfloat16
F32 = jnp.float32

D = 4096
FF = 1536
HD = 128
MROWS = 16
TOPK = 8
CTX = 16
NY = 8
NZ = 8
NXC = 8
SLOTS = 256
ROWS = 192
RB = 48
CB = 384
CHUNK = 6 * RB + 16
SEND_ORDER = [(dy, dx) for dy in (4, 3, 5, 2, 6, 1, 7, 0) for dx in (1, 0) if (dy, dx) != (0, 0)]


def iota(shape, dim):
    return lax.broadcasted_iota(jnp.int32, shape, dim)


def dot(a, b, ca=1, cb=0):
    return lax.dot_general(a, b, (((ca,), (cb,)), ((), ())), preferred_element_type=F32)


def kernel(
    q_hbm, kv_hbm, op_hbm, gain_hbm, ids_hbm, logits_hbm, home_hbm, gu_hbm, dn_hbm, out_ref,
    ids_ref, logits_ref, home_ref, gain_ref,
    kv, op, gu, dn, qall, nb, nr, cs, cr, d1s, d1r, d2s, d2r, rows_ref, tiles_ref, own, xs, xr, ys, yr, acc, fs, hid,
    g1s, g1r, g2s, g2r, picks_ref, combine_ref, perm_ref,
    load_sem, send_sem, q_sem, n_sem, c_sem, d1_sem, d2_sem, x_sem, y_sem, fsend_sem, fy_sem, fx_sem, g1_sem, g2_sem,
):
    e = lax.axis_index("expert")
    c = lax.axis_index("context")
    y, xl = c // 2, c % 2
    core, z, xh = e % 2, (e // 2) % NZ, e // (2 * NZ)
    xc = xh * 2 + core

    loads = [
        pltpu.make_async_copy(src, dst, load_sem.at[i])
        for i, (src, dst) in enumerate(
            [
                (kv_hbm.at[0], kv), (op_hbm, op), (gu_hbm.at[0], gu), (dn_hbm.at[0], dn),
                (q_hbm.at[0], qall.at[c]), (ids_hbm.at[0], ids_ref), (logits_hbm.at[0], logits_ref),
                (home_hbm, home_ref), (gain_hbm, gain_ref),
            ]
        )
    ]
    for i in (5, 6, 7, 4, 8, 0, 1, 2, 3):
        loads[i].start()

    def ctx_peer(dy, dx):
        return ((y + dy) % NY) * 2 + (xl + dx) % 2

    def z_peer(d):
        other = (z + d) % NZ
        return other, (xh * NZ + other) * 2 + core

    def xc_peer(d):
        other = (xc + d) % NXC
        return other, ((other // 2) * NZ + z) * 2 + other % 2

    barrier = pltpu.get_barrier_semaphore()

    def greet(ee, cc):
        pl.semaphore_signal(barrier, inc=1, device_id=(ee, cc), device_id_type=MESH)

    for dy, dx in SEND_ORDER:
        greet(e, ctx_peer(dy, dx))
    for d in range(1, 8):
        greet(z_peer(d)[1], c)
        greet(xc_peer(d)[1], c)

    for i in (5, 6, 7):
        loads[i].wait()
    ids = ids_ref[...]
    raised = jnp.exp(logits_ref[...])
    route = (raised / jnp.sum(raised, axis=0, keepdims=True)).astype(BF).astype(F32)
    expert = iota((64, MROWS), 0)
    chosen = jnp.zeros((64, MROWS), F32)
    weights = jnp.zeros((64, MROWS), F32)
    for j in range(TOPK):
        hit = ids[j : j + 1, :] == expert
        chosen = chosen + jnp.where(hit, 1.0, 0.0)
        weights = weights + jnp.where(hit, route[j : j + 1, :], 0.0)
    r = iota((SLOTS, 64), 0)
    r_xc = (r >> 2) & 7
    r_slot = ((r_xc >> 1) * NZ + (r >> 5)) * 2 + (r_xc & 1)
    lands = jnp.where(home_ref[...] == r_slot, 1.0, 0.0).astype(BF)
    chosen_r = dot(chosen.astype(BF), lands, 0, 1)
    weights_r = dot(weights.astype(BF), lands, 0, 1)
    earlier = jnp.where(iota((MROWS, MROWS), 1) < iota((MROWS, MROWS), 0), 1.0, 0.0).astype(BF)
    rank = dot(earlier, chosen_r.astype(BF))
    right_rank = rank == (iota((MROWS, SLOTS), 1) & 3).astype(F32)
    picks_ref[...] = jnp.where(right_rank, chosen_r, 0.0).astype(BF)
    combine_ref[...] = jnp.where(right_rank, weights_r, 0.0).astype(BF)
    pr, pc = iota((SLOTS, SLOTS), 0), iota((SLOTS, SLOTS), 1)
    perm_ref[...] = jnp.where(pc == ((pr >> 2) & 7) * 32 + (pr >> 5) * 4 + (pr & 3), 1.0, 0.0).astype(BF)

    loads[4].wait()
    loads[8].wait()
    pl.semaphore_wait(barrier, 29)

    def send(src, dst, s_sem, r_sem, ee, cc):
        pltpu.make_async_remote_copy(
            src_ref=src, dst_ref=dst, send_sem=s_sem, recv_sem=r_sem, device_id=(ee, cc), device_id_type=MESH
        ).start()

    def await_bytes(ref, sem):
        pltpu.make_async_copy(ref, ref, sem).wait()

    for dy, dx in SEND_ORDER:
        send(qall.at[c], qall.at[c], send_sem.at[0], q_sem, e, ctx_peer(dy, dx))
    loads[0].wait()
    await_bytes(qall.at[pl.ds(0, 15)], q_sem)

    visible = (iota((128, 128), 0) & 15) >= c
    for g in range(2):
        key, value = kv[:, g * HD : (g + 1) * HD], kv[:, (2 + g) * HD : (3 + g) * HD]
        denoms = []
        for p in range(2):
            query = qall[8 * g : 8 * g + 8, :, p * HD : (p + 1) * HD].reshape(128, HD)
            scores = dot(query, key, 1, 1) * HD ** (-0.5)
            weight = jnp.where(visible, jnp.exp(scores), 0.0)
            denoms.append(jnp.sum(weight, axis=1, keepdims=True))
            numer = dot(weight.astype(BF), value)
            nb[8 * g : 8 * g + 8, :, p * HD : (p + 1) * HD] = numer.astype(BF).reshape(8, MROWS, HD)
        lane = iota((128, 128), 1)
        both = jnp.where(lane < 64, denoms[0], denoms[1])
        high = both.astype(BF).astype(F32)
        packed = jnp.where((lane & 63) < 32, high, both - high)
        nb[8 * g : 8 * g + 8, :, 256:384] = packed.astype(BF).reshape(8, MROWS, 128)

    for dy, dx in SEND_ORDER:
        peer = ctx_peer(dy, dx)
        send(nb.at[peer], nr.at[dy * 2 + dx], send_sem.at[1], n_sem, e, peer)
    nr[0] = nb[c]
    await_bytes(nr.at[pl.ds(1, 15)], n_sem)
    total = nr[0].astype(F32)
    for j in range(1, CTX):
        total = total + nr[j].astype(F32)
    denom0 = total[:, 256:257] + total[:, 288:289]
    denom1 = total[:, 320:321] + total[:, 352:353]
    attended = jnp.concatenate([total[:, 0:128] / denom0, total[:, 128:256] / denom1], axis=1).astype(BF)

    loads[1].wait()
    for dy, dx in SEND_ORDER + [(0, 0)]:
        peer = ctx_peer(dy, dx)
        j = dy * 2 + dx
        part = dot(attended, op[:, pl.ds(pl.multiple_of(peer * 256, 256), 256)]).astype(BF)
        if j == 0:
            cr[0] = part
        else:
            cs[j] = part
            send(cs.at[j], cr.at[j], send_sem.at[2], c_sem, e, peer)
    await_bytes(cr.at[pl.ds(1, 15)], c_sem)
    projected = cr[0].astype(F32)
    for j in range(1, CTX):
        projected = projected + cr[j].astype(F32)
    gain = gain_ref[...]
    normed = (projected * gain).astype(BF)

    d1s[...] = dot(picks_ref[...], normed, 0, 0).astype(BF).reshape(NZ, 32, 256)
    for d in (4, 3, 5, 2, 6, 1, 7):
        other, peer = z_peer(d)
        send(d1s.at[other], d1r.at[z], send_sem.at[3], d1_sem, peer, c)
    d1r[z] = d1s[z]
    await_bytes(d1r.at[pl.ds(0, 7)], d1_sem)
    d2s[...] = dot(perm_ref[...], d1r[...].reshape(SLOTS, 256)).astype(BF).reshape(NXC, 32, 256)
    for d in (4, 3, 5, 2, 6, 1, 7):
        other, peer = xc_peer(d)
        send(d2s.at[other], d2r.at[xc], send_sem.at[4], d2_sem, peer, c)
    d2r[xc] = d2s[xc]
    squeeze = jnp.where(
        iota((ROWS, SLOTS), 1) == (iota((ROWS, SLOTS), 0) & 63) * 4 + (iota((ROWS, SLOTS), 0) >> 6), 1.0, 0.0
    ).astype(BF)
    await_bytes(d2r.at[pl.ds(0, 7)], d2_sem)
    rows32 = dot(squeeze, d2r[...].reshape(SLOTS, 256))
    rows = rows32.astype(BF)

    raw = rows32 * (1.0 / gain)
    squares = jnp.sum(raw * raw, axis=1, keepdims=True)
    rows_ref[...] = rows
    lane16 = iota((16, 128), 1)
    for rb in range(4):
        parts = [squares[rb * RB + t * 16 : rb * RB + t * 16 + 16] for t in range(3)]
        tiles_ref[rb] = jnp.where(lane16 < 32, parts[0], jnp.where(lane16 < 64, parts[1], parts[2])).astype(BF)
    loads[2].wait()
    partner = y * 2 + 1 - xl

    def merge(dy):
        await_bytes(xr.at[dy], x_sem.at[dy])
        both = own[dy].astype(F32) + xr[dy].astype(F32)
        if dy == 0:
            acc[...] = both
        else:
            ys[dy - 1] = both.astype(BF)
            send(ys.at[dy - 1], yr.at[dy - 1], send_sem.at[6], y_sem.at[dy - 1], e, ctx_peer(dy, 0))

    order = (4, 3, 5, 2, 6, 1, 7, 0)
    for n, dy in enumerate(order):
        to = (y + dy) % NY
        low = (to % 2) * 2
        block = [
            rows_ref[pl.ds(pl.multiple_of((low + x) * RB, 16), RB), :] for x in (xl, 1 - xl)
        ]
        left = jnp.concatenate(block, axis=0)
        for half in range(2):
            start = pl.multiple_of(half * FF + (to // 2) * CB, 128)
            part = dot(left, gu[:, pl.ds(start, CB)]).astype(BF)
            for t in range(3):
                at = (half * 3 + t) * RB
                own[dy, at : at + RB, :] = part[0:RB, t * 128 : t * 128 + 128]
                xs[dy, at : at + RB, :] = part[RB : 2 * RB, t * 128 : t * 128 + 128]
        own[dy, 6 * RB : CHUNK, :] = tiles_ref[low + xl]
        xs[dy, 6 * RB : CHUNK, :] = tiles_ref[low + 1 - xl]
        send(xs.at[dy], xr.at[dy], send_sem.at[5], x_sem.at[dy], e, partner)
        if n >= 3:
            merge(order[n - 3])
    for dy in order[5:]:
        merge(dy)
    for dy in (1, 7, 2, 6, 3, 5, 4):
        await_bytes(yr.at[dy - 1], y_sem.at[dy - 1])
        acc[...] += yr[dy - 1].astype(F32)
    scale16 = lax.rsqrt(acc[6 * RB : CHUNK, :] * (1.0 / D) + 1e-06)
    scale = jnp.concatenate([scale16[:, 0:1], scale16[:, 32:33], scale16[:, 64:65]], axis=0)
    for t in range(3):
        gate = acc[t * RB : t * RB + RB, :] * scale
        upper = acc[(3 + t) * RB : (4 + t) * RB, :] * scale
        fs[:, t * 128 : t * 128 + 128] = (gate / (1.0 + jnp.exp(-gate)) * upper).astype(BF)
    def place(cc):
        return hid.at[
            pl.ds(pl.multiple_of((cc % 4) * RB, 16), RB), pl.ds(pl.multiple_of((cc // 4) * CB, 128), CB)
        ]

    near = (1, 7, 2, 6, 3, 5, 4)
    send(fs, place(c), fsend_sem.at[0], fx_sem.at[0], e, partner)
    for dy in near:
        send(fs, place(c), fsend_sem.at[dy], fy_sem.at[dy], e, ctx_peer(dy, 0))
    hid[pl.ds(pl.multiple_of((c % 4) * RB, 16), RB), pl.ds(pl.multiple_of((c // 4) * CB, 128), CB)] = fs[...]
    stretch = jnp.where(
        iota((SLOTS, ROWS), 0) == (iota((SLOTS, ROWS), 1) & 63) * 4 + (iota((SLOTS, ROWS), 1) >> 6), 1.0, 0.0
    ).astype(BF)
    loads[3].wait()
    for dy in near:
        source = place(ctx_peer(NY - dy, 0))
        await_bytes(fs, fy_sem.at[dy])
        send(source, source, fsend_sem.at[NY + dy], fx_sem.at[dy], e, partner)
    for dy in (0,) + near:
        await_bytes(fs, fx_sem.at[dy])
    result = dot(hid[...], dn[...]).astype(BF)

    g1s[...] = dot(stretch, result).astype(BF).reshape(NXC, 32, 256)
    for d in (4, 3, 5, 2, 6, 1, 7):
        other, peer = xc_peer(d)
        send(g1s.at[other], g1r.at[xc], send_sem.at[7], g1_sem, peer, c)
    g1r[xc] = g1s[xc]
    await_bytes(g1r.at[pl.ds(0, 7)], g1_sem)
    g2s[...] = dot(perm_ref[...], g1r[...].reshape(SLOTS, 256)).astype(BF).reshape(NZ, 32, 256)
    for d in (4, 3, 5, 2, 6, 1, 7):
        other, peer = z_peer(d)
        send(g2s.at[other], g2r.at[z], send_sem.at[8], g2_sem, peer, c)
    g2r[z] = g2s[z]
    await_bytes(g2r.at[pl.ds(0, 7)], g2_sem)
    out_ref[0] = dot(combine_ref[...], g2r[...].reshape(SLOTS, 256)).astype(BF)

    await_bytes(qall.at[pl.ds(0, 15)], send_sem.at[0])
    await_bytes(nr.at[pl.ds(0, 15)], send_sem.at[1])
    await_bytes(cr.at[pl.ds(0, 15)], send_sem.at[2])
    await_bytes(d1r.at[pl.ds(0, 7)], send_sem.at[3])
    await_bytes(d2r.at[pl.ds(0, 7)], send_sem.at[4])
    await_bytes(xr, send_sem.at[5])
    await_bytes(yr, send_sem.at[6])
    for j in range(8):
        await_bytes(fs, fsend_sem.at[j])
    for j in range(9, 16):
        await_bytes(fs, fsend_sem.at[j])
    await_bytes(g1r.at[pl.ds(0, 7)], send_sem.at[7])
    await_bytes(g2r.at[pl.ds(0, 7)], send_sem.at[8])


def body(queries, keys_values, out_proj, norm_gain, expert_ids, route_logits, home, gate_up, down):
    vm = pl.BlockSpec(memory_space=pltpu.VMEM)
    hb = pl.BlockSpec(memory_space=pl.ANY)
    dma = pltpu.SemaphoreType.DMA
    vmem = pltpu.VMEM
    return pl.pallas_call(
        kernel,
        out_shape=jax.ShapeDtypeStruct((1, MROWS, 256), BF),
        in_specs=[hb] * 9,
        out_specs=vm,
        scratch_shapes=[
            vmem((TOPK, MROWS), jnp.int32),
            vmem((TOPK, MROWS), F32),
            vmem((1, 64), jnp.int32),
            vmem((1, 256), F32),
            vmem((128, 512), BF),
            vmem((256, D), BF),
            vmem((256, 2 * FF), BF),
            vmem((FF, 256), BF),
            vmem((CTX, MROWS, 256), BF),
            vmem((CTX, MROWS, 384), BF),
            vmem((CTX, MROWS, 384), BF),
            vmem((CTX, MROWS, 256), BF),
            vmem((CTX, MROWS, 256), BF),
            vmem((NZ, 32, 256), BF),
            vmem((NZ, 32, 256), BF),
            vmem((NXC, 32, 256), BF),
            vmem((NXC, 32, 256), BF),
            vmem((ROWS, 256), BF),
            vmem((4, 16, 128), BF),
            vmem((NY, CHUNK, 128), BF),
            vmem((NY, CHUNK, 128), BF),
            vmem((NY, CHUNK, 128), BF),
            vmem((NY - 1, CHUNK, 128), BF),
            vmem((NY - 1, CHUNK, 128), BF),
            vmem((CHUNK, 128), F32),
            vmem((RB, CB), BF),
            vmem((ROWS, FF), BF),
            vmem((NXC, 32, 256), BF),
            vmem((NXC, 32, 256), BF),
            vmem((NZ, 32, 256), BF),
            vmem((NZ, 32, 256), BF),
            vmem((MROWS, SLOTS), BF),
            vmem((MROWS, SLOTS), BF),
            vmem((SLOTS, SLOTS), BF),
            dma((9,)),
            dma((9,)),
            dma, dma, dma, dma, dma,
            dma((NY,)),
            dma((NY - 1,)),
            dma((2 * NY,)),
            dma((NY,)),
            dma((NY,)),
            dma, dma,
        ],
        compiler_params=pltpu.CompilerParams(
            collective_id=0, has_side_effects=True, vmem_limit_bytes=63 * 1024 * 1024
        ),
    )(
        queries, keys_values, out_proj, norm_gain.reshape(1, 256), jnp.swapaxes(expert_ids, 1, 2),
        jnp.swapaxes(route_logits, 1, 2), home.reshape(1, 64), gate_up, down,
    )


def solution(mesh):
    in_specs = (
        P("expert", None, "context"),
        P("expert", "context", None),
        P("context", None),
        P("context"),
        P("expert", None, None),
        P("expert", None, None),
        P(),
        P("expert", "context", None),
        P("expert", None, "context"),
    )
    out_specs = P("expert", None, "context")
    return jax.shard_map(body, mesh=mesh, in_specs=in_specs, out_specs=out_specs, check_vma=False)
```

```python
import functools

import jax
import jax.numpy as jnp
from jax import lax
from jax.experimental import pallas as pl
from jax.experimental.pallas import tpu as pltpu
from jax.sharding import PartitionSpec as P

MESH = pl.DeviceIdType.MESH
BF = jnp.bfloat16
F32 = jnp.float32

D = 4096
FF = 1536
HD = 128
MROWS = 16
TOPK = 8
CTX = 16
NY = 8
NZ = 8
NX = 4
CHIPS = NX * NZ
SLOTS = 256
ROWS = 192
RB = 48
CB = 384
CHUNK = 6 * RB + 16
SEND_ORDER = [(dy, dx) for dy in (4, 3, 5, 2, 6, 1, 7, 0) for dx in (1, 0) if (dy, dx) != (0, 0)]

CHIP_ORDER = sorted(
    [(dx, dz) for dx in range(NX) for dz in range(NZ) if (dx, dz) != (0, 0)],
    key=lambda at: -(2 * min(at[0], NX - at[0]) + min(at[1], NZ - at[1])),
)


def iota(shape, dim):
    return lax.broadcasted_iota(jnp.int32, shape, dim)


def dot(a, b, ca=1, cb=0):
    return lax.dot_general(a, b, (((ca,), (cb,)), ((), ())), preferred_element_type=F32)


def kernel(
    q_hbm, kv_hbm, op_hbm, gain_hbm, ids_hbm, logits_hbm, home_hbm, gu_hbm, dn_hbm, out_ref,
    ids_ref, logits_ref, home_ref, gain_ref,
    kv, op, gu, dn, qall, nb, nr, cs, cr, rows2, ds, dr, rows_ref, tiles_ref, made, xr, ys, yr, yd, held, acc, fs, hid,
    gs, gr, half_s, half_r, tab, tab_s,
    load_sem, send_sem, q_sem, n_sem, c_sem, t_sem, s_sem, d_sem, esend_sem, x_sem, y_sem, fsend_sem, fy_sem, fx_sem, g_sem, h_sem, ring_sem,
):
    e = lax.axis_index("expert")
    c = lax.axis_index("context")
    y, xl = c // 2, c % 2
    core, z, xh = e % 2, (e // 2) % NZ, e // (2 * NZ)
    chip = e // 2
    sibling = chip * 2 + 1 - core
    sign = 1 - 2 * core

    loads = [
        pltpu.make_async_copy(src, dst, load_sem.at[i])
        for i, (src, dst) in enumerate(
            [
                (kv_hbm.at[0], kv), (op_hbm, op), (gu_hbm.at[0], gu), (dn_hbm.at[0], dn),
                (q_hbm.at[0], qall.at[c]), (ids_hbm.at[0], ids_ref), (logits_hbm.at[0], logits_ref),
                (home_hbm, home_ref), (gain_hbm, gain_ref),
            ]
        )
    ]
    for i in (5, 6, 7, 4, 8, 0, 1, 2, 3):
        loads[i].start()

    def ctx_peer(dy, dx):
        return ((y + dy) % NY) * 2 + (xl + dx) % 2

    def y_peer(k):
        return ((y + NY + sign * k) % NY) * 2 + xl

    def chip_peer(dx, dz):
        return ((xh + dx) % NX) * NZ + (z + dz) % NZ

    barrier = pltpu.get_barrier_semaphore()

    def greet(ee, cc):
        pl.semaphore_signal(barrier, inc=1, device_id=(ee, cc), device_id_type=MESH)

    for dy, dx in SEND_ORDER:
        greet(e, ctx_peer(dy, dx))
    for dz in (4, 3, 5, 2, 6, 1, 7):
        greet(chip_peer(0, dz) * 2 + core, c)
    for dx in (2, 1, 3):
        greet(chip_peer(dx, 0) * 2 + core, c)
    greet(sibling, c)
    loads[4].wait()
    pl.semaphore_wait(barrier, 26)

    def send(src, dst, s_sem, r_sem, ee, cc):
        pltpu.make_async_remote_copy(
            src_ref=src, dst_ref=dst, send_sem=s_sem, recv_sem=r_sem, device_id=(ee, cc), device_id_type=MESH
        ).start()

    def await_bytes(ref, sem):
        pltpu.make_async_copy(ref, ref, sem).wait()

    for dy, dx in SEND_ORDER:
        send(qall.at[c], qall.at[c], send_sem.at[0], q_sem, e, ctx_peer(dy, dx))
    for dx in (2, 1, 3):
        pl.semaphore_signal(ring_sem, inc=1, device_id=(chip_peer(dx, 0) * 2 + core, c), device_id_type=MESH)

    for i in (5, 6, 7):
        loads[i].wait()
    ids = ids_ref[...]
    raised = jnp.exp(logits_ref[...])
    route = (raised / jnp.sum(raised, axis=0, keepdims=True)).astype(BF).astype(F32)
    expert = iota((64, MROWS), 0)
    chosen = jnp.zeros((64, MROWS), F32)
    weights = jnp.zeros((64, MROWS), F32)
    for j in range(TOPK):
        hit = ids[j : j + 1, :] == expert
        chosen = chosen + jnp.where(hit, 1.0, 0.0)
        weights = weights + jnp.where(hit, route[j : j + 1, :], 0.0)
    chosen, weights = chosen.astype(BF), weights.astype(BF)
    earlier = jnp.where(iota((MROWS, MROWS), 1) < iota((MROWS, MROWS), 0), 1.0, 0.0).astype(BF)
    column = iota((MROWS, SLOTS), 1)
    wanted = jnp.where(((column >> 2) & 1) == core, column & 3, -1).astype(F32)
    for side in (1, 0):
        at_core = (core + side) % 2
        lands = jnp.where(home_ref[...] == (iota((SLOTS, 64), 0) >> 3) * 2 + at_core, 1.0, 0.0).astype(BF)
        chosen_r = dot(chosen, lands, 0, 1)
        weights_r = dot(weights, lands, 0, 1)
        right_rank = dot(earlier, chosen_r.astype(BF)) == wanted
        both = jnp.concatenate(
            [jnp.where(right_rank, chosen_r, 0.0), jnp.where(right_rank, weights_r, 0.0)], axis=0
        ).astype(BF)
        if side == 1:
            tab_s[...] = both
            send(tab_s, tab.at[core], send_sem.at[3], t_sem, sibling, c)
        else:
            tab[core] = both

    loads[0].wait()
    await_bytes(qall.at[pl.ds(0, 15)], q_sem)

    visible = (iota((128, 128), 0) & 15) >= c
    for g in range(2):
        key, value = kv[:, g * HD : (g + 1) * HD], kv[:, (2 + g) * HD : (3 + g) * HD]
        denoms = []
        for p in range(2):
            query = qall[8 * g : 8 * g + 8, :, p * HD : (p + 1) * HD].reshape(128, HD)
            scores = dot(query, key, 1, 1) * HD ** (-0.5)
            weight = jnp.where(visible, jnp.exp(scores), 0.0)
            denoms.append(jnp.sum(weight, axis=1, keepdims=True))
            numer = dot(weight.astype(BF), value)
            nb[8 * g : 8 * g + 8, :, p * HD : (p + 1) * HD] = numer.astype(BF).reshape(8, MROWS, HD)
        lane = iota((128, 128), 1)
        both = jnp.where(lane < 64, denoms[0], denoms[1])
        high = both.astype(BF).astype(F32)
        packed = jnp.where((lane & 63) < 32, high, both - high)
        nb[8 * g : 8 * g + 8, :, 256:384] = packed.astype(BF).reshape(8, MROWS, 128)

    for dy, dx in SEND_ORDER:
        peer = ctx_peer(dy, dx)
        send(nb.at[peer], nr.at[dy * 2 + dx], send_sem.at[1], n_sem, e, peer)
    nr[0] = nb[c]
    await_bytes(nr.at[pl.ds(1, 15)], n_sem)
    total = nr[0].astype(F32)
    for j in range(1, CTX):
        total = total + nr[j].astype(F32)
    denom0 = total[:, 256:257] + total[:, 288:289]
    denom1 = total[:, 320:321] + total[:, 352:353]
    attended = jnp.concatenate([total[:, 0:128] / denom0, total[:, 128:256] / denom1], axis=1).astype(BF)

    loads[1].wait()
    for dy, dx in SEND_ORDER + [(0, 0)]:
        peer = ctx_peer(dy, dx)
        j = dy * 2 + dx
        part = dot(attended, op[:, pl.ds(pl.multiple_of(peer * 256, 256), 256)]).astype(BF)
        if j == 0:
            cr[0] = part
        else:
            cs[j] = part
            send(cs.at[j], cr.at[j], send_sem.at[2], c_sem, e, peer)
    await_bytes(cr.at[pl.ds(1, 15)], c_sem)
    projected = cr[0].astype(F32)
    for j in range(1, CTX):
        projected = projected + cr[j].astype(F32)
    loads[8].wait()
    gain = gain_ref[...]
    rows2[core] = (projected * gain).astype(BF)

    send(rows2.at[core], rows2.at[core], send_sem.at[4], s_sem, sibling, c)
    squeeze = jnp.where(
        iota((ROWS, SLOTS), 1) == (iota((ROWS, SLOTS), 0) & 63) * 4 + (iota((ROWS, SLOTS), 0) >> 6), 1.0, 0.0
    ).astype(BF)
    await_bytes(tab_s, t_sem)
    picks = tab[:, 0:MROWS, :].reshape(2 * MROWS, SLOTS)
    await_bytes(rows2.at[0], s_sem)
    slot_rows = dot(picks, rows2[...].reshape(2 * MROWS, 256), 0, 0).astype(BF)
    ds[:, 0:8, :] = slot_rows[:, 0:128].reshape(CHIPS, 8, 128)
    ds[:, 8:16, :] = slot_rows[:, 128:256].reshape(CHIPS, 8, 128)
    pl.semaphore_wait(ring_sem, NX - 1)
    for dx, dz in CHIP_ORDER:
        peer = chip_peer(dx, dz)
        send(ds.at[peer], dr.at[chip], send_sem.at[7], d_sem, peer * 2 + core, c)
    dr[chip] = ds[chip]
    await_bytes(dr.at[pl.ds(0, CHIPS - 1)], d_sem)
    arrived = jnp.concatenate(
        [dr[:, 0:8, :].reshape(SLOTS, 128), dr[:, 8:16, :].reshape(SLOTS, 128)], axis=1
    )
    rows32 = dot(squeeze, arrived)
    rows = rows32.astype(BF)

    raw = rows32 * (1.0 / gain)
    squares = jnp.sum(raw * raw, axis=1, keepdims=True)
    rows_ref[...] = rows
    lane16 = iota((16, 128), 1)
    for rb in range(4):
        parts = [squares[rb * RB + t * 16 : rb * RB + t * 16 + 16] for t in range(3)]
        tiles_ref[rb] = jnp.where(lane16 < 32, parts[0], jnp.where(lane16 < 64, parts[1], parts[2])).astype(BF)
    loads[2].wait()
    partner = y * 2 + 1 - xl

    def make(k):
        to = (y + NY + sign * k) % NY
        low = (to % 2) * 2
        block = [rows_ref[pl.ds(pl.multiple_of((low + x) * RB, 16), RB), :] for x in (xl, 1 - xl)]
        left = jnp.concatenate(block, axis=0)
        for half in range(2):
            start = pl.multiple_of(half * FF + (to // 2) * CB, 128)
            part = dot(left, gu[:, pl.ds(start, CB)]).astype(BF)
            for t in range(3):
                at = (half * 3 + t) * RB
                for side in range(2):
                    made[k, side, at : at + RB, :] = part[side * RB : side * RB + RB, t * 128 : t * 128 + 128]
        made[k, 0, 6 * RB : CHUNK, :] = tiles_ref[low + xl]
        made[k, 1, 6 * RB : CHUNK, :] = tiles_ref[low + 1 - xl]

    def send_x(src, n):
        send(src, xr.at[n], esend_sem.at[n], x_sem.at[n], e, partner)

    def take_x(n):
        await_bytes(xr.at[n], x_sem.at[n])
        return xr[n].astype(F32)

    def send_y(n, value, k):
        ys[n] = value.astype(BF)
        send(ys.at[n], yr.at[n], esend_sem.at[6 + n], y_sem.at[n], e, y_peer(k))

    def take_y(n):
        await_bytes(yr.at[n], y_sem.at[n])
        return yr[n].astype(F32)

    def send_pair(n, k, steps):
        send(made.at[k], yd.at[n], esend_sem.at[11 + n], y_sem.at[5 + n], e, y_peer(steps))

    def mine(k):
        return made[k, 0].astype(F32)

    make(4)
    send_x(made.at[4, 1], 0)
    make(3)
    send_x(made.at[3, 1], 1)
    make(5)
    send_x(made.at[5, 1], 2)
    make(1)
    send_pair(0, 1, 1)
    make(2)
    send_x(made.at[2, 1], 3)
    make(7)
    send_pair(1, 7, -1)
    make(6)
    send_x(made.at[6, 1], 4)
    send_y(0, mine(4) + take_x(0), 2)
    make(0)
    send_y(1, mine(3) + take_x(1), 1)
    send_y(2, mine(5) + take_x(2), -1)
    for n in range(2):
        await_bytes(yd.at[n], y_sem.at[5 + n])
    held[...] = (made[0, 1].astype(F32) + yd[0, 1].astype(F32) + yd[1, 1].astype(F32)).astype(BF)
    send_x(held, 5)
    acc[...] = mine(0) + yd[0, 0].astype(F32) + yd[1, 0].astype(F32)
    send_y(3, mine(2) + take_x(3) + take_y(0) + take_y(1), 2)
    send_y(4, mine(6) + take_x(4) + take_y(2), -2)
    acc[...] += take_x(5)
    acc[...] += take_y(3) + take_y(4)
    scale16 = lax.rsqrt(acc[6 * RB : CHUNK, :] * (1.0 / D) + 1e-06)
    scale = jnp.concatenate([scale16[:, 0:1], scale16[:, 32:33], scale16[:, 64:65]], axis=0)
    for t in range(3):
        gate = acc[t * RB : t * RB + RB, :] * scale
        upper = acc[(3 + t) * RB : (4 + t) * RB, :] * scale
        fs[:, t * 128 : t * 128 + 128] = (gate / (1.0 + jnp.exp(-gate)) * upper).astype(BF)
    def place(cc):
        return hid.at[
            pl.ds(pl.multiple_of((cc % 4) * RB, 16), RB), pl.ds(pl.multiple_of((cc // 4) * CB, 128), CB)
        ]

    def there(k):
        return place(y_peer(k))

    def across(k):
        return place(y_peer(k) + 1 - 2 * xl)

    def pass_on(n, src, dst, sems, k, peer):
        send(src, dst, fsend_sem.at[n], sems.at[k + 3], e, peer)

    pass_on(0, fs, place(c), fx_sem, 0, partner)
    pass_on(1, fs, place(c), fy_sem, -2, y_peer(2))
    pass_on(2, fs, place(c), fy_sem, 2, y_peer(-2))
    pass_on(3, fs, place(c), fy_sem, -1, y_peer(1))
    pass_on(4, fs, place(c), fy_sem, 1, y_peer(-1))
    hid[pl.ds(pl.multiple_of((c % 4) * RB, 16), RB), pl.ds(pl.multiple_of((c // 4) * CB, 128), CB)] = fs[...]
    stretch = jnp.where(
        iota((SLOTS, ROWS), 0) == (iota((SLOTS, ROWS), 1) & 63) * 4 + (iota((SLOTS, ROWS), 1) >> 6), 1.0, 0.0
    ).astype(BF)
    loads[3].wait()
    await_bytes(fs, fx_sem.at[3])
    pass_on(5, across(0), across(0), fx_sem, -1, y_peer(1))
    pass_on(6, across(0), across(0), fx_sem, 1, y_peer(-1))
    await_bytes(fs, fy_sem.at[1])
    pass_on(7, there(-2), there(-2), fy_sem, 4, y_peer(2))
    pass_on(8, there(-2), there(-2), fy_sem, -3, y_peer(1))
    pass_on(9, there(-2), there(-2), fx_sem, -2, partner)
    await_bytes(fs, fy_sem.at[5])
    pass_on(10, there(2), there(2), fy_sem, 3, y_peer(-1))
    pass_on(11, there(2), there(2), fx_sem, 2, partner)
    for n, k in ((12, -3), (13, 3), (14, 4)):
        await_bytes(fs, fy_sem.at[k + 3])
        pass_on(n, there(k), there(k), fx_sem, k, partner)
    for k in (-1, 1):
        await_bytes(fs, fy_sem.at[k + 3])
    for k in (-1, 1, -2, 2, -3, 3, 4):
        await_bytes(fs, fx_sem.at[k + 3])
    result = dot(hid[...], dn[...]).astype(BF)

    back = dot(stretch, result).astype(BF)
    gs[:, 0:8, :] = back[:, 0:128].reshape(CHIPS, 8, 128)
    gs[:, 8:16, :] = back[:, 128:256].reshape(CHIPS, 8, 128)
    for dx, dz in CHIP_ORDER:
        peer = chip_peer(dx, dz)
        send(gs.at[peer], gr.at[chip], send_sem.at[8], g_sem, peer * 2 + core, c)
    gr[chip] = gs[chip]
    combine = tab[:, MROWS : 2 * MROWS, :].reshape(2 * MROWS, SLOTS)
    await_bytes(gr.at[pl.ds(0, CHIPS - 1)], g_sem)
    returned = jnp.concatenate(
        [gr[:, 0:8, :].reshape(SLOTS, 128), gr[:, 8:16, :].reshape(SLOTS, 128)], axis=1
    )
    half_s[...] = dot(combine, returned).reshape(2, MROWS, 256)
    send(half_s.at[1 - core], half_r, send_sem.at[9], h_sem, sibling, c)
    await_bytes(half_r, h_sem)
    out_ref[0] = (half_s[core] + half_r[...]).astype(BF)

    await_bytes(qall.at[pl.ds(0, 15)], send_sem.at[0])
    await_bytes(nr.at[pl.ds(0, 15)], send_sem.at[1])
    await_bytes(cr.at[pl.ds(0, 15)], send_sem.at[2])
    await_bytes(tab_s, send_sem.at[3])
    await_bytes(rows2.at[0], send_sem.at[4])
    for n in range(11):
        await_bytes(held, esend_sem.at[n])
    for n in range(2):
        await_bytes(yd.at[n], esend_sem.at[11 + n])
    for n in range(15):
        await_bytes(fs, fsend_sem.at[n])
    await_bytes(dr.at[pl.ds(0, CHIPS - 1)], send_sem.at[7])
    await_bytes(gr.at[pl.ds(0, CHIPS - 1)], send_sem.at[8])
    await_bytes(half_r, send_sem.at[9])


def body(queries, keys_values, out_proj, norm_gain, expert_ids, route_logits, home, gate_up, down):
    vm = pl.BlockSpec(memory_space=pltpu.VMEM)
    hb = pl.BlockSpec(memory_space=pl.ANY)
    dma = pltpu.SemaphoreType.DMA
    vmem = pltpu.VMEM
    return pl.pallas_call(
        kernel,
        out_shape=jax.ShapeDtypeStruct((1, MROWS, 256), BF),
        in_specs=[hb] * 9,
        out_specs=vm,
        scratch_shapes=[
            vmem((TOPK, MROWS), jnp.int32),
            vmem((TOPK, MROWS), F32),
            vmem((1, 64), jnp.int32),
            vmem((1, 256), F32),
            vmem((128, 512), BF),
            vmem((256, D), BF),
            vmem((256, 2 * FF), BF),
            vmem((FF, 256), BF),
            vmem((CTX, MROWS, 256), BF),
            vmem((CTX, MROWS, 384), BF),
            vmem((CTX, MROWS, 384), BF),
            vmem((CTX, MROWS, 256), BF),
            vmem((CTX, MROWS, 256), BF),
            vmem((2, MROWS, 256), BF),
            vmem((CHIPS, 16, 128), BF),
            vmem((CHIPS, 16, 128), BF),
            vmem((ROWS, 256), BF),
            vmem((4, 16, 128), BF),
            vmem((NY, 2, CHUNK, 128), BF),
            vmem((6, CHUNK, 128), BF),
            vmem((5, CHUNK, 128), BF),
            vmem((5, CHUNK, 128), BF),
            vmem((2, 2, CHUNK, 128), BF),
            vmem((CHUNK, 128), BF),
            vmem((CHUNK, 128), F32),
            vmem((RB, CB), BF),
            vmem((ROWS, FF), BF),
            vmem((CHIPS, 16, 128), BF),
            vmem((CHIPS, 16, 128), BF),
            vmem((2, MROWS, 256), F32),
            vmem((MROWS, 256), F32),
            vmem((2, 2 * MROWS, SLOTS), BF),
            vmem((2 * MROWS, SLOTS), BF),
            dma((9,)),
            dma((10,)),
            dma, dma, dma, dma, dma, dma,
            dma((13,)),
            dma((6,)),
            dma((7,)),
            dma((15,)),
            dma((NY,)),
            dma((NY,)),
            dma, dma,
            pltpu.SemaphoreType.REGULAR,
        ],
        compiler_params=pltpu.CompilerParams(
            collective_id=0, has_side_effects=True, vmem_limit_bytes=63 * 1024 * 1024
        ),
    )(
        queries, keys_values, out_proj, norm_gain.reshape(1, 256), jnp.swapaxes(expert_ids, 1, 2),
        jnp.swapaxes(route_logits, 1, 2), home.reshape(1, 64), gate_up, down,
    )


def solution(mesh):
    in_specs = (
        P("expert", None, "context"),
        P("expert", "context", None),
        P("context", None),
        P("context"),
        P("expert", None, None),
        P("expert", None, None),
        P(),
        P("expert", "context", None),
        P("expert", None, "context"),
    )
    out_specs = P("expert", None, "context")
    return jax.shard_map(body, mesh=mesh, in_specs=in_specs, out_specs=out_specs, check_vma=False)
```

```python
import functools

import jax
import jax.numpy as jnp
from jax import lax
from jax.experimental import pallas as pl
from jax.experimental.pallas import tpu as pltpu
from jax.sharding import PartitionSpec as P

MESH = pl.DeviceIdType.MESH
BF = jnp.bfloat16
F32 = jnp.float32

D = 4096
FF = 1536
HD = 128
MROWS = 16
TOPK = 8
CTX = 16
NY = 8
NZ = 8
NX = 4
CHIPS = NX * NZ
SLOTS = 256
ROWS = 192
RB = 48
CB = 384
CHUNK = 6 * RB + 16
SEND_ORDER = [(dy, dx) for dy in (4, 3, 5, 2, 6, 1, 7, 0) for dx in (1, 0) if (dy, dx) != (0, 0)]

CHIP_ORDER = sorted(
    [(dx, dz) for dx in range(NX) for dz in range(NZ) if (dx, dz) != (0, 0)],
    key=lambda at: -(2 * min(at[0], NX - at[0]) + min(at[1], NZ - at[1])),
)


def iota(shape, dim):
    return lax.broadcasted_iota(jnp.int32, shape, dim)


def dot(a, b, ca=1, cb=0):
    return lax.dot_general(a, b, (((ca,), (cb,)), ((), ())), preferred_element_type=F32)


def kernel(
    q_hbm, kv_hbm, op_hbm, gain_hbm, ids_hbm, logits_hbm, home_hbm, gu_hbm, dn_hbm, out_ref,
    ids_ref, logits_ref, home_ref, gain_ref,
    kv, op, gu, dn, qall, nb, nr, cs, cr, rows2, ds, dr, rows_ref, tiles_ref, made, xr, ys, yr, yd, held, acc, fs, hid,
    gs, gr, half_s, half_r, tab, tab_s,
    load_sem, send_sem, q_sem, n_sem, c_sem, t_sem, s_sem, d_sem, esend_sem, x_sem, y_sem, fsend_sem, fy_sem, fx_sem, g_sem, h_sem, ring_sem,
):
    e = lax.axis_index("expert")
    c = lax.axis_index("context")
    y, xl = c // 2, c % 2
    core, z, xh = e % 2, (e // 2) % NZ, e // (2 * NZ)
    chip = e // 2
    sibling = chip * 2 + 1 - core
    sign = 1 - 2 * core

    loads = [
        pltpu.make_async_copy(src, dst, load_sem.at[i])
        for i, (src, dst) in enumerate(
            [
                (kv_hbm.at[0], kv), (op_hbm, op), (gu_hbm.at[0], gu), (dn_hbm.at[0], dn),
                (q_hbm.at[0], qall.at[c]), (ids_hbm.at[0], ids_ref), (logits_hbm.at[0], logits_ref),
                (home_hbm, home_ref), (gain_hbm, gain_ref),
            ]
        )
    ]
    for i in (5, 6, 7, 4, 8, 0, 1, 2, 3):
        loads[i].start()

    def ctx_peer(dy, dx):
        return ((y + dy) % NY) * 2 + (xl + dx) % 2

    def y_peer(k):
        return ((y + NY + sign * k) % NY) * 2 + xl

    def chip_peer(dx, dz):
        return ((xh + dx) % NX) * NZ + (z + dz) % NZ

    barrier = pltpu.get_barrier_semaphore()

    def greet(ee, cc):
        pl.semaphore_signal(barrier, inc=1, device_id=(ee, cc), device_id_type=MESH)

    for dy, dx in SEND_ORDER:
        greet(e, ctx_peer(dy, dx))
    for dz in (4, 3, 5, 2, 6, 1, 7):
        greet(chip_peer(0, dz) * 2 + core, c)
    for dx in (2, 1, 3):
        greet(chip_peer(dx, 0) * 2 + core, c)
    greet(sibling, c)
    loads[4].wait()
    pl.semaphore_wait(barrier, 26)

    def send(src, dst, s_sem, r_sem, ee, cc):
        pltpu.make_async_remote_copy(
            src_ref=src, dst_ref=dst, send_sem=s_sem, recv_sem=r_sem, device_id=(ee, cc), device_id_type=MESH
        ).start()

    def await_bytes(ref, sem):
        pltpu.make_async_copy(ref, ref, sem).wait()

    for dy, dx in SEND_ORDER:
        send(qall.at[c], qall.at[c], send_sem.at[0], q_sem, e, ctx_peer(dy, dx))
    for dx in (2, 1, 3):
        pl.semaphore_signal(ring_sem, inc=1, device_id=(chip_peer(dx, 0) * 2 + core, c), device_id_type=MESH)

    for i in (5, 6, 7):
        loads[i].wait()
    ids = ids_ref[...]
    raised = jnp.exp(logits_ref[...])
    route = (raised / jnp.sum(raised, axis=0, keepdims=True)).astype(BF).astype(F32)
    expert = iota((64, MROWS), 0)
    chosen = jnp.zeros((64, MROWS), F32)
    weights = jnp.zeros((64, MROWS), F32)
    for j in range(TOPK):
        hit = ids[j : j + 1, :] == expert
        chosen = chosen + jnp.where(hit, 1.0, 0.0)
        weights = weights + jnp.where(hit, route[j : j + 1, :], 0.0)
    chosen, weights = chosen.astype(BF), weights.astype(BF)
    earlier = jnp.where(iota((MROWS, MROWS), 1) < iota((MROWS, MROWS), 0), 1.0, 0.0).astype(BF)
    column = iota((MROWS, SLOTS), 1)
    wanted = jnp.where(((column >> 2) & 1) == core, column & 3, -1).astype(F32)
    for side in (1, 0):
        at_core = (core + side) % 2
        lands = jnp.where(home_ref[...] == (iota((SLOTS, 64), 0) >> 3) * 2 + at_core, 1.0, 0.0).astype(BF)
        chosen_r = dot(chosen, lands, 0, 1)
        weights_r = dot(weights, lands, 0, 1)
        right_rank = dot(earlier, chosen_r.astype(BF)) == wanted
        both = jnp.concatenate(
            [jnp.where(right_rank, chosen_r, 0.0), jnp.where(right_rank, weights_r, 0.0)], axis=0
        ).astype(BF)
        if side == 1:
            tab_s[...] = both
            send(tab_s, tab.at[core], send_sem.at[3], t_sem, sibling, c)
        else:
            tab[core] = both

    loads[0].wait()
    await_bytes(qall.at[pl.ds(0, 15)], q_sem)

    visible = (iota((128, 128), 0) & 15) >= c
    lane = iota((128, 128), 1)
    for far in (1, 0):
        g = (y // 4 + far) % 2
        key = kv[:, pl.ds(pl.multiple_of(g * HD, HD), HD)]
        value = kv[:, pl.ds(pl.multiple_of((2 + g) * HD, HD), HD)]
        heads = pl.ds(pl.multiple_of(8 * g, 8), 8)
        denoms = []
        for p in range(2):
            query = qall[heads, :, p * HD : (p + 1) * HD].reshape(128, HD)
            scores = dot(query, key, 1, 1) * HD ** (-0.5)
            weight = jnp.where(visible, jnp.exp(scores), 0.0)
            denoms.append(jnp.sum(weight, axis=1, keepdims=True))
            numer = dot(weight.astype(BF), value)
            nb[heads, :, p * HD : (p + 1) * HD] = numer.astype(BF).reshape(8, MROWS, HD)
        both = jnp.where(lane < 64, denoms[0], denoms[1])
        high = both.astype(BF).astype(F32)
        packed = jnp.where((lane & 63) < 32, high, both - high)
        nb[heads, :, 256:384] = packed.astype(BF).reshape(8, MROWS, 128)
        for step in (0, 3, 1, 2) if far else (2, 1, 3, 0):
            for dx in (1, 0):
                if far or (step, dx) != (0, 0):
                    peer = (4 * g + (y + step) % 4) * 2 + (xl + dx) % 2
                    send(nb.at[peer], nr.at[c], send_sem.at[1], n_sem, e, peer)
    nr[c] = nb[c]
    await_bytes(nr.at[pl.ds(1, 15)], n_sem)
    total = nr[0].astype(F32)
    for j in range(1, CTX):
        total = total + nr[j].astype(F32)
    denom0 = total[:, 256:257] + total[:, 288:289]
    denom1 = total[:, 320:321] + total[:, 352:353]
    attended = jnp.concatenate([total[:, 0:128] / denom0, total[:, 128:256] / denom1], axis=1).astype(BF)

    loads[1].wait()
    for dy, dx in SEND_ORDER + [(0, 0)]:
        peer = ctx_peer(dy, dx)
        j = dy * 2 + dx
        part = dot(attended, op[:, pl.ds(pl.multiple_of(peer * 256, 256), 256)]).astype(BF)
        if j == 0:
            cr[0] = part
        else:
            cs[j] = part
            send(cs.at[j], cr.at[j], send_sem.at[2], c_sem, e, peer)
    await_bytes(cr.at[pl.ds(1, 15)], c_sem)
    projected = cr[0].astype(F32)
    for j in range(1, CTX):
        projected = projected + cr[j].astype(F32)
    loads[8].wait()
    gain = gain_ref[...]
    rows2[core] = (projected * gain).astype(BF)

    send(rows2.at[core], rows2.at[core], send_sem.at[4], s_sem, sibling, c)
    squeeze = jnp.where(
        iota((ROWS, SLOTS), 1) == (iota((ROWS, SLOTS), 0) & 63) * 4 + (iota((ROWS, SLOTS), 0) >> 6), 1.0, 0.0
    ).astype(BF)
    await_bytes(tab_s, t_sem)
    picks = tab[:, 0:MROWS, :].reshape(2 * MROWS, SLOTS)
    await_bytes(rows2.at[0], s_sem)
    slot_rows = dot(picks, rows2[...].reshape(2 * MROWS, 256), 0, 0).astype(BF)
    ds[:, 0:8, :] = slot_rows[:, 0:128].reshape(CHIPS, 8, 128)
    ds[:, 8:16, :] = slot_rows[:, 128:256].reshape(CHIPS, 8, 128)
    pl.semaphore_wait(ring_sem, NX - 1)
    for dx, dz in CHIP_ORDER:
        peer = chip_peer(dx, dz)
        send(ds.at[peer], dr.at[chip], send_sem.at[7], d_sem, peer * 2 + core, c)
    dr[chip] = ds[chip]
    await_bytes(dr.at[pl.ds(0, CHIPS - 1)], d_sem)
    arrived = jnp.concatenate(
        [dr[:, 0:8, :].reshape(SLOTS, 128), dr[:, 8:16, :].reshape(SLOTS, 128)], axis=1
    )
    rows32 = dot(squeeze, arrived)
    rows = rows32.astype(BF)

    raw = rows32 * (1.0 / gain)
    squares = jnp.sum(raw * raw, axis=1, keepdims=True)
    rows_ref[...] = rows
    lane16 = iota((16, 128), 1)
    for rb in range(4):
        parts = [squares[rb * RB + t * 16 : rb * RB + t * 16 + 16] for t in range(3)]
        tiles_ref[rb] = jnp.where(lane16 < 32, parts[0], jnp.where(lane16 < 64, parts[1], parts[2])).astype(BF)
    loads[2].wait()
    partner = y * 2 + 1 - xl

    def make(k):
        to = (y + NY + sign * k) % NY
        low = (to % 2) * 2
        block = [rows_ref[pl.ds(pl.multiple_of((low + x) * RB, 16), RB), :] for x in (xl, 1 - xl)]
        left = jnp.concatenate(block, axis=0)
        for half in range(2):
            start = pl.multiple_of(half * FF + (to // 2) * CB, 128)
            part = dot(left, gu[:, pl.ds(start, CB)]).astype(BF)
            for t in range(3):
                at = (half * 3 + t) * RB
                for side in range(2):
                    made[k, side, at : at + RB, :] = part[side * RB : side * RB + RB, t * 128 : t * 128 + 128]
        made[k, 0, 6 * RB : CHUNK, :] = tiles_ref[low + xl]
        made[k, 1, 6 * RB : CHUNK, :] = tiles_ref[low + 1 - xl]

    def send_x(src, n):
        send(src, xr.at[n], esend_sem.at[n], x_sem.at[n], e, partner)

    def take_x(n):
        await_bytes(xr.at[n], x_sem.at[n])
        return xr[n].astype(F32)

    def send_y(n, value, k):
        ys[n] = value.astype(BF)
        send(ys.at[n], yr.at[n], esend_sem.at[6 + n], y_sem.at[n], e, y_peer(k))

    def take_y(n):
        await_bytes(yr.at[n], y_sem.at[n])
        return yr[n].astype(F32)

    def send_pair(n, k, steps):
        send(made.at[k], yd.at[n], esend_sem.at[11 + n], y_sem.at[5 + n], e, y_peer(steps))

    def mine(k):
        return made[k, 0].astype(F32)

    make(4)
    send_x(made.at[4, 1], 0)
    make(3)
    send_x(made.at[3, 1], 1)
    make(5)
    send_x(made.at[5, 1], 2)
    make(1)
    send_pair(0, 1, 1)
    make(2)
    send_x(made.at[2, 1], 3)
    make(7)
    send_pair(1, 7, -1)
    make(6)
    send_x(made.at[6, 1], 4)
    send_y(0, mine(4) + take_x(0), 2)
    make(0)
    send_y(1, mine(3) + take_x(1), 1)
    send_y(2, mine(5) + take_x(2), -1)
    for n in range(2):
        await_bytes(yd.at[n], y_sem.at[5 + n])
    held[...] = (made[0, 1].astype(F32) + yd[0, 1].astype(F32) + yd[1, 1].astype(F32)).astype(BF)
    send_x(held, 5)
    acc[...] = mine(0) + yd[0, 0].astype(F32) + yd[1, 0].astype(F32)
    send_y(3, mine(2) + take_x(3) + take_y(0) + take_y(1), 2)
    send_y(4, mine(6) + take_x(4) + take_y(2), -2)
    acc[...] += take_x(5)
    acc[...] += take_y(3) + take_y(4)
    scale16 = lax.rsqrt(acc[6 * RB : CHUNK, :] * (1.0 / D) + 1e-06)
    scale = jnp.concatenate([scale16[:, 0:1], scale16[:, 32:33], scale16[:, 64:65]], axis=0)
    for t in range(3):
        gate = acc[t * RB : t * RB + RB, :] * scale
        upper = acc[(3 + t) * RB : (4 + t) * RB, :] * scale
        fs[:, t * 128 : t * 128 + 128] = (gate / (1.0 + jnp.exp(-gate)) * upper).astype(BF)
    def place(cc):
        return hid.at[
            pl.ds(pl.multiple_of((cc % 4) * RB, 16), RB), pl.ds(pl.multiple_of((cc // 4) * CB, 128), CB)
        ]

    def there(k):
        return place(y_peer(k))

    def across(k):
        return place(y_peer(k) + 1 - 2 * xl)

    def pass_on(n, src, dst, sems, k, peer):
        send(src, dst, fsend_sem.at[n], sems.at[k + 3], e, peer)

    pass_on(0, fs, place(c), fx_sem, 0, partner)
    pass_on(1, fs, place(c), fy_sem, -2, y_peer(2))
    pass_on(2, fs, place(c), fy_sem, 2, y_peer(-2))
    pass_on(3, fs, place(c), fy_sem, -1, y_peer(1))
    pass_on(4, fs, place(c), fy_sem, 1, y_peer(-1))
    hid[pl.ds(pl.multiple_of((c % 4) * RB, 16), RB), pl.ds(pl.multiple_of((c // 4) * CB, 128), CB)] = fs[...]
    stretch = jnp.where(
        iota((SLOTS, ROWS), 0) == (iota((SLOTS, ROWS), 1) & 63) * 4 + (iota((SLOTS, ROWS), 1) >> 6), 1.0, 0.0
    ).astype(BF)
    loads[3].wait()
    await_bytes(fs, fx_sem.at[3])
    pass_on(5, across(0), across(0), fx_sem, -1, y_peer(1))
    pass_on(6, across(0), across(0), fx_sem, 1, y_peer(-1))
    await_bytes(fs, fy_sem.at[1])
    pass_on(7, there(-2), there(-2), fy_sem, 4, y_peer(2))
    pass_on(8, there(-2), there(-2), fy_sem, -3, y_peer(1))
    pass_on(9, there(-2), there(-2), fx_sem, -2, partner)
    await_bytes(fs, fy_sem.at[5])
    pass_on(10, there(2), there(2), fy_sem, 3, y_peer(-1))
    pass_on(11, there(2), there(2), fx_sem, 2, partner)
    for n, k in ((12, -3), (13, 3), (14, 4)):
        await_bytes(fs, fy_sem.at[k + 3])
        pass_on(n, there(k), there(k), fx_sem, k, partner)
    for k in (-1, 1):
        await_bytes(fs, fy_sem.at[k + 3])
    for k in (-1, 1, -2, 2, -3, 3, 4):
        await_bytes(fs, fx_sem.at[k + 3])
    result = dot(hid[...], dn[...]).astype(BF)

    back = dot(stretch, result).astype(BF)
    gs[:, 0:8, :] = back[:, 0:128].reshape(CHIPS, 8, 128)
    gs[:, 8:16, :] = back[:, 128:256].reshape(CHIPS, 8, 128)
    for dx, dz in CHIP_ORDER:
        peer = chip_peer(dx, dz)
        send(gs.at[peer], gr.at[chip], send_sem.at[8], g_sem, peer * 2 + core, c)
    gr[chip] = gs[chip]
    combine = tab[:, MROWS : 2 * MROWS, :].reshape(2 * MROWS, SLOTS)
    await_bytes(gr.at[pl.ds(0, CHIPS - 1)], g_sem)
    returned = jnp.concatenate(
        [gr[:, 0:8, :].reshape(SLOTS, 128), gr[:, 8:16, :].reshape(SLOTS, 128)], axis=1
    )
    half_s[...] = dot(combine, returned).reshape(2, MROWS, 256)
    send(half_s.at[1 - core], half_r, send_sem.at[9], h_sem, sibling, c)
    await_bytes(half_r, h_sem)
    out_ref[0] = (half_s[core] + half_r[...]).astype(BF)

    await_bytes(qall.at[pl.ds(0, 15)], send_sem.at[0])
    await_bytes(nr.at[pl.ds(0, 15)], send_sem.at[1])
    await_bytes(cr.at[pl.ds(0, 15)], send_sem.at[2])
    await_bytes(tab_s, send_sem.at[3])
    await_bytes(rows2.at[0], send_sem.at[4])
    for n in range(11):
        await_bytes(held, esend_sem.at[n])
    for n in range(2):
        await_bytes(yd.at[n], esend_sem.at[11 + n])
    for n in range(15):
        await_bytes(fs, fsend_sem.at[n])
    await_bytes(dr.at[pl.ds(0, CHIPS - 1)], send_sem.at[7])
    await_bytes(gr.at[pl.ds(0, CHIPS - 1)], send_sem.at[8])
    await_bytes(half_r, send_sem.at[9])


def body(queries, keys_values, out_proj, norm_gain, expert_ids, route_logits, home, gate_up, down):
    vm = pl.BlockSpec(memory_space=pltpu.VMEM)
    hb = pl.BlockSpec(memory_space=pl.ANY)
    dma = pltpu.SemaphoreType.DMA
    vmem = pltpu.VMEM
    return pl.pallas_call(
        kernel,
        out_shape=jax.ShapeDtypeStruct((1, MROWS, 256), BF),
        in_specs=[hb] * 9,
        out_specs=vm,
        scratch_shapes=[
            vmem((TOPK, MROWS), jnp.int32),
            vmem((TOPK, MROWS), F32),
            vmem((1, 64), jnp.int32),
            vmem((1, 256), F32),
            vmem((128, 512), BF),
            vmem((256, D), BF),
            vmem((256, 2 * FF), BF),
            vmem((FF, 256), BF),
            vmem((CTX, MROWS, 256), BF),
            vmem((CTX, MROWS, 384), BF),
            vmem((CTX, MROWS, 384), BF),
            vmem((CTX, MROWS, 256), BF),
            vmem((CTX, MROWS, 256), BF),
            vmem((2, MROWS, 256), BF),
            vmem((CHIPS, 16, 128), BF),
            vmem((CHIPS, 16, 128), BF),
            vmem((ROWS, 256), BF),
            vmem((4, 16, 128), BF),
            vmem((NY, 2, CHUNK, 128), BF),
            vmem((6, CHUNK, 128), BF),
            vmem((5, CHUNK, 128), BF),
            vmem((5, CHUNK, 128), BF),
            vmem((2, 2, CHUNK, 128), BF),
            vmem((CHUNK, 128), BF),
            vmem((CHUNK, 128), F32),
            vmem((RB, CB), BF),
            vmem((ROWS, FF), BF),
            vmem((CHIPS, 16, 128), BF),
            vmem((CHIPS, 16, 128), BF),
            vmem((2, MROWS, 256), F32),
            vmem((MROWS, 256), F32),
            vmem((2, 2 * MROWS, SLOTS), BF),
            vmem((2 * MROWS, SLOTS), BF),
            dma((9,)),
            dma((10,)),
            dma, dma, dma, dma, dma, dma,
            dma((13,)),
            dma((6,)),
            dma((7,)),
            dma((15,)),
            dma((NY,)),
            dma((NY,)),
            dma, dma,
            pltpu.SemaphoreType.REGULAR,
        ],
        compiler_params=pltpu.CompilerParams(
            collective_id=0, has_side_effects=True, vmem_limit_bytes=63 * 1024 * 1024
        ),
    )(
        queries, keys_values, out_proj, norm_gain.reshape(1, 256), jnp.swapaxes(expert_ids, 1, 2),
        jnp.swapaxes(route_logits, 1, 2), home.reshape(1, 64), gate_up, down,
    )


def solution(mesh):
    in_specs = (
        P("expert", None, "context"),
        P("expert", "context", None),
        P("context", None),
        P("context"),
        P("expert", None, None),
        P("expert", None, None),
        P(),
        P("expert", "context", None),
        P("expert", None, "context"),
    )
    out_specs = P("expert", None, "context")
    return jax.shard_map(body, mesh=mesh, in_specs=in_specs, out_specs=out_specs, check_vma=False)
```

```python
import functools

import jax
import jax.numpy as jnp
from jax import lax
from jax.experimental import pallas as pl
from jax.experimental.pallas import tpu as pltpu
from jax.sharding import PartitionSpec as P

MESH = pl.DeviceIdType.MESH
BF = jnp.bfloat16
F32 = jnp.float32

D = 4096
FF = 1536
HD = 128
MROWS = 16
TOPK = 8
CTX = 16
NY = 8
NZ = 8
NX = 4
CHIPS = NX * NZ
SLOTS = 256
ROWS = 192
RB = 48
CB = 384
CHUNK = 6 * RB + 16
PARTS = ((0, 3 * RB), (3 * RB, 3 * RB + 16))
SEND_ORDER = [(dy, dx) for dy in (4, 3, 5, 2, 6, 1, 7, 0) for dx in (1, 0) if (dy, dx) != (0, 0)]

CHIP_ORDER = sorted(
    [(dx, dz) for dx in range(NX) for dz in range(NZ) if (dx, dz) != (0, 0)],
    key=lambda at: -(2 * min(at[0], NX - at[0]) + min(at[1], NZ - at[1])),
)


def iota(shape, dim):
    return lax.broadcasted_iota(jnp.int32, shape, dim)


def dot(a, b, ca=1, cb=0):
    return lax.dot_general(a, b, (((ca,), (cb,)), ((), ())), preferred_element_type=F32)


def kernel(
    q_hbm, kv_hbm, op_hbm, gain_hbm, ids_hbm, logits_hbm, home_hbm, gu_hbm, dn_hbm, out_ref,
    ids_ref, logits_ref, home_ref, gain_ref,
    kv, op, gu, dn, qall, nb, nr, cs, cr, rows2, ds, dr, rows_ref, tiles_ref, made, xr, ys, yr, yd, held, acc, fs, hid,
    gs, gr, half_s, half_r, tab, tab_s,
    load_sem, send_sem, q_sem, n_sem, c_sem, t_sem, s_sem, d_sem, esend_sem, x_sem, y_sem, fsend_sem, fy_sem, fx_sem, g_sem, h_sem, ring_sem,
):
    e = lax.axis_index("expert")
    c = lax.axis_index("context")
    y, xl = c // 2, c % 2
    core, z, xh = e % 2, (e // 2) % NZ, e // (2 * NZ)
    chip = e // 2
    sibling = chip * 2 + 1 - core
    sign = 1 - 2 * core

    loads = [
        pltpu.make_async_copy(src, dst, load_sem.at[i])
        for i, (src, dst) in enumerate(
            [
                (kv_hbm.at[0], kv), (op_hbm, op), (gu_hbm.at[0], gu), (dn_hbm.at[0], dn),
                (q_hbm.at[0], qall.at[c]), (ids_hbm.at[0], ids_ref), (logits_hbm.at[0], logits_ref),
                (home_hbm, home_ref), (gain_hbm, gain_ref),
            ]
        )
    ]
    for i in (5, 6, 7, 4, 8, 0, 1, 2, 3):
        loads[i].start()

    def ctx_peer(dy, dx):
        return ((y + dy) % NY) * 2 + (xl + dx) % 2

    def y_peer(k):
        return ((y + NY + sign * k) % NY) * 2 + xl

    def chip_peer(dx, dz):
        return ((xh + dx) % NX) * NZ + (z + dz) % NZ

    barrier = pltpu.get_barrier_semaphore()

    def greet(ee, cc):
        pl.semaphore_signal(barrier, inc=1, device_id=(ee, cc), device_id_type=MESH)

    for dy, dx in SEND_ORDER:
        greet(e, ctx_peer(dy, dx))
    for dz in (4, 3, 5, 2, 6, 1, 7):
        greet(chip_peer(0, dz) * 2 + core, c)
    for dx in (2, 1, 3):
        greet(chip_peer(dx, 0) * 2 + core, c)
    greet(sibling, c)
    loads[4].wait()
    pl.semaphore_wait(barrier, 26)

    def send(src, dst, s_sem, r_sem, ee, cc):
        pltpu.make_async_remote_copy(
            src_ref=src, dst_ref=dst, send_sem=s_sem, recv_sem=r_sem, device_id=(ee, cc), device_id_type=MESH
        ).start()

    def await_bytes(ref, sem):
        pltpu.make_async_copy(ref, ref, sem).wait()

    for dy, dx in SEND_ORDER:
        send(qall.at[c], qall.at[c], send_sem.at[0], q_sem, e, ctx_peer(dy, dx))
    for dx in (2, 1, 3):
        pl.semaphore_signal(ring_sem, inc=1, device_id=(chip_peer(dx, 0) * 2 + core, c), device_id_type=MESH)

    for i in (5, 6, 7):
        loads[i].wait()
    ids = ids_ref[...]
    raised = jnp.exp(logits_ref[...])
    route = (raised / jnp.sum(raised, axis=0, keepdims=True)).astype(BF).astype(F32)
    expert = iota((64, MROWS), 0)
    chosen = jnp.zeros((64, MROWS), F32)
    weights = jnp.zeros((64, MROWS), F32)
    for j in range(TOPK):
        hit = ids[j : j + 1, :] == expert
        chosen = chosen + jnp.where(hit, 1.0, 0.0)
        weights = weights + jnp.where(hit, route[j : j + 1, :], 0.0)
    chosen, weights = chosen.astype(BF), weights.astype(BF)
    earlier = jnp.where(iota((MROWS, MROWS), 1) < iota((MROWS, MROWS), 0), 1.0, 0.0).astype(BF)
    column = iota((MROWS, SLOTS), 1)
    wanted = jnp.where(((column >> 2) & 1) == core, column & 3, -1).astype(F32)
    for side in (1, 0):
        at_core = (core + side) % 2
        lands = jnp.where(home_ref[...] == (iota((SLOTS, 64), 0) >> 3) * 2 + at_core, 1.0, 0.0).astype(BF)
        chosen_r = dot(chosen, lands, 0, 1)
        weights_r = dot(weights, lands, 0, 1)
        right_rank = dot(earlier, chosen_r.astype(BF)) == wanted
        both = jnp.concatenate(
            [jnp.where(right_rank, chosen_r, 0.0), jnp.where(right_rank, weights_r, 0.0)], axis=0
        ).astype(BF)
        if side == 1:
            tab_s[...] = both
            send(tab_s, tab.at[core], send_sem.at[3], t_sem, sibling, c)
        else:
            tab[core] = both

    loads[0].wait()
    await_bytes(qall.at[pl.ds(0, 15)], q_sem)

    visible = (iota((128, 128), 0) & 15) >= c
    lane = iota((128, 128), 1)
    for far in (1, 0):
        g = (y // 4 + far) % 2
        key = kv[:, pl.ds(pl.multiple_of(g * HD, HD), HD)]
        value = kv[:, pl.ds(pl.multiple_of((2 + g) * HD, HD), HD)]
        heads = pl.ds(pl.multiple_of(8 * g, 8), 8)
        denoms = []
        for p in range(2):
            query = qall[heads, :, p * HD : (p + 1) * HD].reshape(128, HD)
            scores = dot(query, key, 1, 1) * HD ** (-0.5)
            weight = jnp.where(visible, jnp.exp(scores), 0.0)
            denoms.append(jnp.sum(weight, axis=1, keepdims=True))
            numer = dot(weight.astype(BF), value)
            nb[heads, :, p * HD : (p + 1) * HD] = numer.astype(BF).reshape(8, MROWS, HD)
        both = jnp.where(lane < 64, denoms[0], denoms[1])
        high = both.astype(BF).astype(F32)
        packed = jnp.where((lane & 63) < 32, high, both - high)
        nb[heads, :, 256:384] = packed.astype(BF).reshape(8, MROWS, 128)
        for step in (0, 3, 1, 2) if far else (2, 1, 3, 0):
            for dx in (1, 0):
                if far or (step, dx) != (0, 0):
                    peer = (4 * g + (y + step) % 4) * 2 + (xl + dx) % 2
                    send(nb.at[peer], nr.at[c], send_sem.at[1], n_sem, e, peer)
    nr[c] = nb[c]
    await_bytes(nr.at[pl.ds(1, 15)], n_sem)
    total = nr[0].astype(F32)
    for j in range(1, CTX):
        total = total + nr[j].astype(F32)
    denom0 = total[:, 256:257] + total[:, 288:289]
    denom1 = total[:, 320:321] + total[:, 352:353]
    attended = jnp.concatenate([total[:, 0:128] / denom0, total[:, 128:256] / denom1], axis=1).astype(BF)

    loads[1].wait()
    for dy, dx in SEND_ORDER + [(0, 0)]:
        peer = ctx_peer(dy, dx)
        j = dy * 2 + dx
        part = dot(attended, op[:, pl.ds(pl.multiple_of(peer * 256, 256), 256)]).astype(BF)
        if j == 0:
            cr[0] = part
        else:
            cs[j] = part
            send(cs.at[j], cr.at[j], send_sem.at[2], c_sem, e, peer)
    await_bytes(cr.at[pl.ds(1, 15)], c_sem)
    projected = cr[0].astype(F32)
    for j in range(1, CTX):
        projected = projected + cr[j].astype(F32)
    loads[8].wait()
    gain = gain_ref[...]
    rows2[core] = (projected * gain).astype(BF)

    send(rows2.at[core], rows2.at[core], send_sem.at[4], s_sem, sibling, c)
    squeeze = jnp.where(
        iota((ROWS, SLOTS), 1) == (iota((ROWS, SLOTS), 0) & 63) * 4 + (iota((ROWS, SLOTS), 0) >> 6), 1.0, 0.0
    ).astype(BF)
    await_bytes(tab_s, t_sem)
    picks = tab[:, 0:MROWS, :].reshape(2 * MROWS, SLOTS)
    await_bytes(rows2.at[0], s_sem)
    slot_rows = dot(picks, rows2[...].reshape(2 * MROWS, 256), 0, 0).astype(BF)
    ds[:, 0:8, :] = slot_rows[:, 0:128].reshape(CHIPS, 8, 128)
    ds[:, 8:16, :] = slot_rows[:, 128:256].reshape(CHIPS, 8, 128)
    pl.semaphore_wait(ring_sem, NX - 1)
    for dx, dz in CHIP_ORDER:
        peer = chip_peer(dx, dz)
        send(ds.at[peer], dr.at[chip], send_sem.at[7], d_sem, peer * 2 + core, c)
    dr[chip] = ds[chip]
    await_bytes(dr.at[pl.ds(0, CHIPS - 1)], d_sem)
    arrived = jnp.concatenate(
        [dr[:, 0:8, :].reshape(SLOTS, 128), dr[:, 8:16, :].reshape(SLOTS, 128)], axis=1
    )
    rows32 = dot(squeeze, arrived)
    rows = rows32.astype(BF)

    raw = rows32 * (1.0 / gain)
    squares = jnp.sum(raw * raw, axis=1, keepdims=True)
    rows_ref[...] = rows
    lane16 = iota((16, 128), 1)
    for rb in range(4):
        parts = [squares[rb * RB + t * 16 : rb * RB + t * 16 + 16] for t in range(3)]
        tiles_ref[rb] = jnp.where(lane16 < 32, parts[0], jnp.where(lane16 < 64, parts[1], parts[2])).astype(BF)
    loads[2].wait()
    partner = y * 2 + 1 - xl

    def make(k):
        to = (y + NY + sign * k) % NY
        low = (to % 2) * 2
        block = [rows_ref[pl.ds(pl.multiple_of((low + x) * RB, 16), RB), :] for x in (xl, 1 - xl)]
        left = jnp.concatenate(block, axis=0)
        for half in range(2):
            start = pl.multiple_of(half * FF + (to // 2) * CB, 128)
            part = dot(left, gu[:, pl.ds(start, CB)]).astype(BF)
            for t in range(3):
                at = (half * 3 + t) * RB
                for side in range(2):
                    made[k, side, at : at + RB, :] = part[side * RB : side * RB + RB, t * 128 : t * 128 + 128]
        made[k, 0, 6 * RB : CHUNK, :] = tiles_ref[low + xl]
        made[k, 1, 6 * RB : CHUNK, :] = tiles_ref[low + 1 - xl]

    def send_x(src, n, p):
        at = pl.ds(*PARTS[p])
        send(src.at[at], xr.at[n, at], esend_sem.at[2 * n + p], x_sem.at[2 * n + p], e, partner)

    def take_x(n, p):
        at = pl.ds(*PARTS[p])
        await_bytes(xr.at[n, at], x_sem.at[2 * n + p])
        return xr[n, at].astype(F32)

    def send_y(n, p, value, k):
        at = pl.ds(*PARTS[p])
        ys[n, at] = value.astype(BF)
        send(ys.at[n, at], yr.at[n, at], esend_sem.at[12 + 2 * n + p], y_sem.at[2 * n + p], e, y_peer(k))

    def take_y(n, p):
        at = pl.ds(*PARTS[p])
        await_bytes(yr.at[n, at], y_sem.at[2 * n + p])
        return yr[n, at].astype(F32)

    def send_pair(n, k, steps):
        send(made.at[k], yd.at[n], esend_sem.at[22 + n], y_sem.at[10 + n], e, y_peer(steps))

    def mine(k, p):
        return made[k, 0, pl.ds(*PARTS[p])].astype(F32)

    def make_x(k, n):
        make(k)
        for p in range(2):
            send_x(made.at[k, 1], n, p)

    make_x(4, 0)
    make_x(3, 1)
    make_x(5, 2)
    make(1)
    send_pair(0, 1, 1)
    make_x(2, 3)
    make(7)
    send_pair(1, 7, -1)
    make_x(6, 4)
    for p in range(2):
        send_y(0, p, mine(4, p) + take_x(0, p), 2)
    make(0)
    for p in range(2):
        send_y(1, p, mine(3, p) + take_x(1, p), 1)
    for p in range(2):
        send_y(2, p, mine(5, p) + take_x(2, p), -1)
    for n in range(2):
        await_bytes(yd.at[n], y_sem.at[10 + n])
    held[...] = (made[0, 1].astype(F32) + yd[0, 1].astype(F32) + yd[1, 1].astype(F32)).astype(BF)
    for p in range(2):
        send_x(held, 5, p)
    acc[...] = made[0, 0].astype(F32) + yd[0, 0].astype(F32) + yd[1, 0].astype(F32)
    for p in range(2):
        send_y(3, p, mine(2, p) + take_x(3, p) + take_y(0, p) + take_y(1, p), 2)
    for p in range(2):
        send_y(4, p, mine(6, p) + take_x(4, p) + take_y(2, p), -2)
    for p in range(2):
        acc[pl.ds(*PARTS[p])] += take_x(5, p)
    for p in range(2):
        acc[pl.ds(*PARTS[p])] += take_y(3, p) + take_y(4, p)
    scale16 = lax.rsqrt(acc[6 * RB : CHUNK, :] * (1.0 / D) + 1e-06)
    scale = jnp.concatenate([scale16[:, 0:1], scale16[:, 32:33], scale16[:, 64:65]], axis=0)
    for t in range(3):
        gate = acc[t * RB : t * RB + RB, :] * scale
        upper = acc[(3 + t) * RB : (4 + t) * RB, :] * scale
        fs[:, t * 128 : t * 128 + 128] = (gate / (1.0 + jnp.exp(-gate)) * upper).astype(BF)
    def place(cc):
        return hid.at[
            pl.ds(pl.multiple_of((cc % 4) * RB, 16), RB), pl.ds(pl.multiple_of((cc // 4) * CB, 128), CB)
        ]

    def there(k):
        return place(y_peer(k))

    def across(k):
        return place(y_peer(k) + 1 - 2 * xl)

    def pass_on(n, src, dst, sems, k, peer):
        send(src, dst, fsend_sem.at[n], sems.at[k + 3], e, peer)

    pass_on(0, fs, place(c), fx_sem, 0, partner)
    pass_on(1, fs, place(c), fy_sem, -2, y_peer(2))
    pass_on(2, fs, place(c), fy_sem, 2, y_peer(-2))
    pass_on(3, fs, place(c), fy_sem, -1, y_peer(1))
    pass_on(4, fs, place(c), fy_sem, 1, y_peer(-1))
    hid[pl.ds(pl.multiple_of((c % 4) * RB, 16), RB), pl.ds(pl.multiple_of((c // 4) * CB, 128), CB)] = fs[...]
    stretch = jnp.where(
        iota((SLOTS, ROWS), 0) == (iota((SLOTS, ROWS), 1) & 63) * 4 + (iota((SLOTS, ROWS), 1) >> 6), 1.0, 0.0
    ).astype(BF)
    loads[3].wait()
    await_bytes(fs, fx_sem.at[3])
    pass_on(5, across(0), across(0), fx_sem, -1, y_peer(1))
    pass_on(6, across(0), across(0), fx_sem, 1, y_peer(-1))
    await_bytes(fs, fy_sem.at[1])
    pass_on(7, there(-2), there(-2), fy_sem, 4, y_peer(2))
    pass_on(8, there(-2), there(-2), fy_sem, -3, y_peer(1))
    pass_on(9, there(-2), there(-2), fx_sem, -2, partner)
    await_bytes(fs, fy_sem.at[5])
    pass_on(10, there(2), there(2), fy_sem, 3, y_peer(-1))
    pass_on(11, there(2), there(2), fx_sem, 2, partner)
    for n, k in ((12, -3), (13, 3), (14, 4)):
        await_bytes(fs, fy_sem.at[k + 3])
        pass_on(n, there(k), there(k), fx_sem, k, partner)
    for k in (-1, 1):
        await_bytes(fs, fy_sem.at[k + 3])
    for k in (-1, 1, -2, 2, -3, 3, 4):
        await_bytes(fs, fx_sem.at[k + 3])
    result = dot(hid[...], dn[...]).astype(BF)

    back = dot(stretch, result).astype(BF)
    gs[:, 0:8, :] = back[:, 0:128].reshape(CHIPS, 8, 128)
    gs[:, 8:16, :] = back[:, 128:256].reshape(CHIPS, 8, 128)
    for dx, dz in CHIP_ORDER:
        peer = chip_peer(dx, dz)
        send(gs.at[peer], gr.at[chip], send_sem.at[8], g_sem, peer * 2 + core, c)
    gr[chip] = gs[chip]
    combine = tab[:, MROWS : 2 * MROWS, :].reshape(2 * MROWS, SLOTS)
    await_bytes(gr.at[pl.ds(0, CHIPS - 1)], g_sem)
    returned = jnp.concatenate(
        [gr[:, 0:8, :].reshape(SLOTS, 128), gr[:, 8:16, :].reshape(SLOTS, 128)], axis=1
    )
    half_s[...] = dot(combine, returned).reshape(2, MROWS, 256)
    send(half_s.at[1 - core], half_r, send_sem.at[9], h_sem, sibling, c)
    await_bytes(half_r, h_sem)
    out_ref[0] = (half_s[core] + half_r[...]).astype(BF)

    await_bytes(qall.at[pl.ds(0, 15)], send_sem.at[0])
    await_bytes(nr.at[pl.ds(0, 15)], send_sem.at[1])
    await_bytes(cr.at[pl.ds(0, 15)], send_sem.at[2])
    await_bytes(tab_s, send_sem.at[3])
    await_bytes(rows2.at[0], send_sem.at[4])
    for n in range(11):
        for p in range(2):
            await_bytes(held.at[pl.ds(*PARTS[p])], esend_sem.at[2 * n + p])
    for n in range(2):
        await_bytes(yd.at[n], esend_sem.at[22 + n])
    for n in range(15):
        await_bytes(fs, fsend_sem.at[n])
    await_bytes(dr.at[pl.ds(0, CHIPS - 1)], send_sem.at[7])
    await_bytes(gr.at[pl.ds(0, CHIPS - 1)], send_sem.at[8])
    await_bytes(half_r, send_sem.at[9])


def body(queries, keys_values, out_proj, norm_gain, expert_ids, route_logits, home, gate_up, down):
    vm = pl.BlockSpec(memory_space=pltpu.VMEM)
    hb = pl.BlockSpec(memory_space=pl.ANY)
    dma = pltpu.SemaphoreType.DMA
    vmem = pltpu.VMEM
    return pl.pallas_call(
        kernel,
        out_shape=jax.ShapeDtypeStruct((1, MROWS, 256), BF),
        in_specs=[hb] * 9,
        out_specs=vm,
        scratch_shapes=[
            vmem((TOPK, MROWS), jnp.int32),
            vmem((TOPK, MROWS), F32),
            vmem((1, 64), jnp.int32),
            vmem((1, 256), F32),
            vmem((128, 512), BF),
            vmem((256, D), BF),
            vmem((256, 2 * FF), BF),
            vmem((FF, 256), BF),
            vmem((CTX, MROWS, 256), BF),
            vmem((CTX, MROWS, 384), BF),
            vmem((CTX, MROWS, 384), BF),
            vmem((CTX, MROWS, 256), BF),
            vmem((CTX, MROWS, 256), BF),
            vmem((2, MROWS, 256), BF),
            vmem((CHIPS, 16, 128), BF),
            vmem((CHIPS, 16, 128), BF),
            vmem((ROWS, 256), BF),
            vmem((4, 16, 128), BF),
            vmem((NY, 2, CHUNK, 128), BF),
            vmem((6, CHUNK, 128), BF),
            vmem((5, CHUNK, 128), BF),
            vmem((5, CHUNK, 128), BF),
            vmem((2, 2, CHUNK, 128), BF),
            vmem((CHUNK, 128), BF),
            vmem((CHUNK, 128), F32),
            vmem((RB, CB), BF),
            vmem((ROWS, FF), BF),
            vmem((CHIPS, 16, 128), BF),
            vmem((CHIPS, 16, 128), BF),
            vmem((2, MROWS, 256), F32),
            vmem((MROWS, 256), F32),
            vmem((2, 2 * MROWS, SLOTS), BF),
            vmem((2 * MROWS, SLOTS), BF),
            dma((9,)),
            dma((10,)),
            dma, dma, dma, dma, dma, dma,
            dma((24,)),
            dma((12,)),
            dma((12,)),
            dma((15,)),
            dma((NY,)),
            dma((NY,)),
            dma, dma,
            pltpu.SemaphoreType.REGULAR,
        ],
        compiler_params=pltpu.CompilerParams(
            collective_id=0, has_side_effects=True, vmem_limit_bytes=63 * 1024 * 1024
        ),
    )(
        queries, keys_values, out_proj, norm_gain.reshape(1, 256), jnp.swapaxes(expert_ids, 1, 2),
        jnp.swapaxes(route_logits, 1, 2), home.reshape(1, 64), gate_up, down,
    )


def solution(mesh):
    in_specs = (
        P("expert", None, "context"),
        P("expert", "context", None),
        P("context", None),
        P("context"),
        P("expert", None, None),
        P("expert", None, None),
        P(),
        P("expert", "context", None),
        P("expert", None, "context"),
    )
    out_specs = P("expert", None, "context")
    return jax.shard_map(body, mesh=mesh, in_specs=in_specs, out_specs=out_specs, check_vma=False)
```
